128 devices in a mesh: freq: 32 (over z, x_lo, y), pair: 4 (over x_hi, core).
Axes of the slice: x: 4 (x_hi: 2, x_lo: 2; x = x_hi * 2 + x_lo), y: 4, z: 4, core: 2. Of those that a mesh axis runs over, the one named last changes fastest.
Arguments:
- voltages: bfloat16 [2048, 50304], P(('freq', 'pair')), may hold values from -90 to 90
- input_alive_mask: int32 [2048], P(('freq', 'pair')), may hold values 0 or 1
- pair_table: int32 [36, 2], P('pair'), may hold values from 0 to 7, as said below
Outputs:
- visibilities: bfloat16 [36, 96, 2, 256, 256], P('pair', 'freq')
The draws below stay inside these ranges and needn't reach their ends.
Inputs may be any that keep to these rules, and one draw needn't show every extreme that they name: `pair_table`: each row holds a row block a and a column block b of the 8 blocks with a <= b; every such pair stands in exactly one row.
All inputs are finite; a program needn't handle non-finite values. No bound on the sum of `input_alive_mask` on one device may be relied on, other than what follows from the above.
Results may differ from the reference program's by a relative error of at most 0.0055.
Values may be sent and summed in bfloat16 or wider, within the bound.
A program may use at most 64 MiB of HBM per device.

```python
import math
import jax
import jax.numpy as jnp
import numpy as np
from jax import lax

INPUTS = 2048
CHAN = 192
BAND = 96
TAPS = 4
SPECTRA = 128
ANTENNA_BLOCKS = 8
BLOCK_INPUTS = 256
PAIR_BLOCKS = 36
VOLTAGE_SAMPLES = 50304


def draw_voltages(key, part):
    key = jax.random.fold_in(key, 11)
    key_gain, key_env, key_noise = jax.random.split(key, 3)
    frames = SPECTRA + TAPS - 1
    period = 2 * CHAN
    input_gains = jnp.exp(jax.random.uniform(key_gain, (INPUTS, 1, 1), jnp.float32, math.log(0.3), math.log(3.0)))
    envelope = jnp.exp(jax.random.uniform(key_env, (1, frames, 1), jnp.float32, math.log(0.5), math.log(5.0)))
    core = jnp.clip(jax.random.normal(key_noise, (INPUTS, frames, period), jnp.float32), -6.0, 6.0)
    return (input_gains * envelope * core).reshape(INPUTS, frames * period).astype(jnp.bfloat16)


def draw_pair_table(key, part):
    key = jax.random.fold_in(key, 23)
    ordering = jax.random.permutation(key, PAIR_BLOCKS)
    upper_triangle = np.triu_indices(ANTENNA_BLOCKS)
    row_blocks = jnp.asarray(upper_triangle[0], dtype=jnp.int32)[ordering]
    col_blocks = jnp.asarray(upper_triangle[1], dtype=jnp.int32)[ordering]
    return jnp.stack([row_blocks, col_blocks], axis=1).astype(jnp.int32)


def touch_ends(array, rng, low, top_value):
    longest = array.shape.index(max(array.shape))
    spots = []
    for shift in (0, 1):
        where = [jax.random.randint(jax.random.fold_in(rng, axis), (), 0, length) for axis, length in enumerate(array.shape)]
        where[longest] = (where[longest] + shift) % array.shape[longest]
        spots.append(tuple(where))
    return array.at[spots[0]].set(low).at[spots[1]].set(top_value)


def setup_inputs(seed: int = 0) -> dict:
    seeds = jax.random.split(jax.random.key(seed), 4)
    voltages = draw_voltages(jax.random.fold_in(seeds[3], 71), 0)
    input_alive_mask = touch_ends((jax.random.randint(seeds[1], (INPUTS,), 0, 16) < 15).astype(jnp.int32), jax.random.fold_in(seeds[1], 1), 0, 1)
    pair_table = draw_pair_table(jax.random.fold_in(seeds[3], 71), 0)
    return dict(voltages=voltages, input_alive_mask=input_alive_mask, pair_table=pair_table)


def filter_window(tap_count, period):
    length = tap_count * period
    sample_index = jnp.arange(length, dtype=jnp.float32)
    shape_part = jnp.sinc((sample_index - length / 2 + 0.5) / period)
    tapering = 0.54 - 0.46 * jnp.cos(2.0 * math.pi * sample_index / (length - 1))
    return (shape_part * tapering).reshape(tap_count, period)

def channelize(block_volts, block_live):
    period = 2 * CHAN
    samples = block_volts.astype(jnp.float32).reshape(BLOCK_INPUTS, SPECTRA + TAPS - 1, period)
    window = filter_window(TAPS, period)
    filtered = window[0] * samples[:, 0:SPECTRA, :]
    for tap_index in range(1, TAPS):
        filtered = filtered + window[tap_index] * samples[:, tap_index:tap_index + SPECTRA, :]
    spectrum = jnp.fft.rfft(filtered, axis=-1)[:, :, :BAND]
    real_part = jnp.transpose(jnp.real(spectrum), (2, 0, 1))
    imag_part = jnp.transpose(jnp.imag(spectrum), (2, 0, 1))
    band_power = lax.optimization_barrier(jnp.mean(real_part * real_part + imag_part * imag_part, axis=2))
    gains = lax.rsqrt(band_power + 1e-06) * block_live.astype(jnp.float32)[None, :]
    return (jnp.stack([real_part, imag_part]) * gains[None, :, :, None]).astype(jnp.bfloat16)

def reference(voltages, input_alive_mask, pair_table):
    voltage_blocks = voltages.reshape(ANTENNA_BLOCKS, BLOCK_INPUTS, VOLTAGE_SAMPLES)
    working_blocks = input_alive_mask.reshape(ANTENNA_BLOCKS, BLOCK_INPUTS)

    def one_block(pieces):
        return channelize(pieces[0], pieces[1])
    equalized = lax.map(one_block, (voltage_blocks, working_blocks))
    inverse = 1.0 / SPECTRA

    def correlate(pair_row):
        row_data = lax.dynamic_index_in_dim(equalized, pair_row[0], 0, keepdims=False).astype(jnp.float32)
        col_data = lax.dynamic_index_in_dim(equalized, pair_row[1], 0, keepdims=False).astype(jnp.float32)
        real_part = jnp.einsum('cks,cls->ckl', row_data[0], col_data[0]) + jnp.einsum('cks,cls->ckl', row_data[1], col_data[1])
        imag_part = jnp.einsum('cks,cls->ckl', row_data[1], col_data[0]) - jnp.einsum('cks,cls->ckl', row_data[0], col_data[1])
        return (jnp.stack([real_part, imag_part], axis=1) * inverse).astype(jnp.bfloat16)
    return lax.map(correlate, pair_table)
```

```python
import functools
import math

import jax
import jax.numpy as jnp
import numpy as np
from jax import lax
from jax.experimental import pallas as pl
from jax.experimental.pallas import tpu as pltpu
from jax.sharding import PartitionSpec as P

CHAN = 192
BAND = 96
TAPS = 4
SPECTRA = 128
BLOCK = 256
PERIOD = 2 * CHAN
SIDE = 4
RINGS = SIDE * SIDE
LOCAL = 16
DEPTH = 3
GROUPS = BAND // DEPTH
MESH = pl.DeviceIdType.MESH

ORDER = (
    (1, 0), (0, 1), (3, 0), (0, 3), (2, 0), (0, 2), (1, 1), (3, 3),
    (1, 3), (3, 1), (2, 1), (1, 2), (2, 3), (3, 2), (2, 2),
)


def tables():
    length = TAPS * PERIOD
    j = np.arange(length, dtype=np.float64)
    window = np.sinc((j - length / 2 + 0.5) / PERIOD) * (0.54 - 0.46 * np.cos(2 * math.pi * j / (length - 1)))
    window = window.reshape(TAPS, PERIOD).astype(np.float32)
    z, y, q, ch = np.meshgrid(np.arange(4), np.arange(4), np.arange(2), np.arange(DEPTH), indexing="ij")
    k = ((z * 8 + q * 4 + y) * DEPTH + ch).reshape(-1)
    phase = 2 * math.pi / PERIOD * (k[:, None] * np.arange(PERIOD)[None, :] % PERIOD)
    rows = np.stack([np.cos(phase), -np.sin(phase)], axis=1).reshape(2 * BAND, PERIOD)
    high = rows.astype(jnp.bfloat16)
    low = (rows - high.astype(np.float64)).astype(jnp.bfloat16)
    return window, np.concatenate([high, low, high], axis=1)


def place():
    f, p = lax.axis_index("freq"), lax.axis_index("pair")
    z, x_lo, y = lax.div(f, 8), lax.rem(lax.div(f, 4), 2), lax.rem(f, 4)
    return z, lax.div(p, 2) * 2 + x_lo, y, lax.rem(p, 2)


def device(z, x, y, c):
    return (z * 8 + lax.rem(x, 2) * 4 + y, lax.div(x, 2) * 2 + c)


def slot(z, x, y, c):
    f, p = device(z, x, y, c)
    return f * 4 + p


def ahead(a, d):
    return lax.rem(a + d, SIDE)


def behind(a, d):
    return lax.rem(a + SIDE - d, SIDE)


def channelize(volts, window, dft, mask, fir, spec, ready):
    def filt(step, carry):
        first = step * 8
        frames = []
        for t in range(8 + TAPS - 1):
            at = pl.multiple_of((first + t) * PERIOD, 128)
            frames.append(volts[:, pl.ds(at, PERIOD)].astype(jnp.float32))
        for t in range(8):
            total = window[0:1, :] * frames[t]
            for m in range(1, TAPS):
                total = total + window[m : m + 1, :] * frames[t + m]
            row = pl.multiple_of((first + t) * LOCAL, LOCAL)
            for j in range(3):
                fir[j, pl.ds(row, LOCAL), :] = total[:, j * 128 : (j + 1) * 128]
        return carry

    lax.fori_loop(0, SPECTRA // 8, filt, 0)

    def transform(pair, carry):
        highs, lows = [], []
        for half in range(2):
            i = pair * 2 + half
            x = jnp.concatenate([fir[j, pl.ds(i, SPECTRA, stride=LOCAL), :] for j in range(3)], axis=1)
            high = x.astype(jnp.bfloat16)
            highs.append(high)
            lows.append((x - high.astype(jnp.float32)).astype(jnp.bfloat16))
        high, low = jnp.concatenate(highs, axis=0), jnp.concatenate(lows, axis=0)
        right = jnp.concatenate([high, high, low], axis=1)
        out = lax.dot_general(dft[...], right, (((1,), (1,)), ((), ())), preferred_element_type=jnp.float32)
        for half in range(2):
            i = pair * 2 + half
            spec[pl.ds(i, 2 * BAND, stride=LOCAL), :] = out[:, half * SPECTRA : (half + 1) * SPECTRA]
        return carry

    lax.fori_loop(0, LOCAL // 2, transform, 0)
    alive = mask[...].astype(jnp.float32)

    def equalize(ring, carry):
        for e in range(2 * DEPTH):
            at = pl.multiple_of((ring * 2 * DEPTH + e) * 2 * LOCAL, 2 * LOCAL)
            re, im = spec[pl.ds(at, LOCAL), :], spec[pl.ds(at + LOCAL, LOCAL), :]
            power = jnp.sum(re * re + im * im, axis=1, keepdims=True) * (1.0 / SPECTRA)
            gain = lax.rsqrt(power + 1e-06) * alive
            both = jnp.concatenate([re * gain, im * gain], axis=1)
            ready[ring, e // DEPTH, e % DEPTH] = both.astype(jnp.bfloat16)
        return carry

    lax.fori_loop(0, RINGS, equalize, 0)


def exchange_kernel(volts, window, dft, mask, out, fir, spec, ready, relay, s1, r1, s2, r2, s3, r3, sl):
    z, x, y, c = place()
    q = lax.rem(x, 2)
    barrier = pltpu.get_barrier_semaphore()
    peers = [device(ahead(z, dz), x, ahead(y, dy), c) for dz, dy in ORDER]
    peers += [device(z, ahead(x, d), y, c) for d in (1, 2, 3)] + [device(z, x, y, 1 - c)]
    for peer in peers:
        pl.semaphore_signal(barrier, inc=1, device_id=peer, device_id_type=MESH)

    channelize(volts, window, dft, mask, fir, spec, ready)

    pl.semaphore_wait(barrier, len(peers))
    sends = []

    def send(src, dst, send_sem, recv_sem, to):
        copy = pltpu.make_async_remote_copy(
            src_ref=src, dst_ref=dst, send_sem=send_sem, recv_sem=recv_sem, device_id=to, device_id_type=MESH
        )
        copy.start()
        sends.append(copy)

    def arrived(dst, sem):
        pltpu.make_async_copy(dst, dst, sem).wait()

    def spread(k, zs, ys, mine, others):
        at = slot(zs, x, ys, c)
        send(others, out.at[at], s2.at[3 * k + 1], r2.at[3 * k + 1], device(z, ahead(x, 1), y, c))
        send(others, out.at[at], s2.at[3 * k + 2], r2.at[3 * k + 2], device(z, ahead(x, 3), y, c))
        send(mine, out.at[at], s2.at[3 * k], r2.at[3 * k], device(z, ahead(x, 2), y, c))
        send(mine, out.at[at], s3.at[4 * k], r3.at[4 * k], device(z, x, y, 1 - c))

    here, own = z * SIDE + y, slot(z, x, y, c)
    spread(0, z, y, ready.at[here, q], ready.at[here, 1 - q])
    keep = pltpu.make_async_copy(ready.at[here, q], out.at[own], sl)
    keep.start()
    for k, (dz, dy) in enumerate(ORDER, 1):
        zd, yd = ahead(z, dz), ahead(y, dy)
        to, there = device(zd, x, yd, c), zd * SIDE + yd
        send(ready.at[there, 1 - q], relay.at[here], s1.at[2 * k + 1], r1.at[2 * k + 1], to)
        send(ready.at[there, q], out.at[own], s1.at[2 * k], r1.at[2 * k], to)
    for k, (dz, dy) in enumerate(ORDER, 1):
        zs, ys = behind(z, dz), behind(y, dy)
        at, ring = slot(zs, x, ys, c), zs * SIDE + ys
        arrived(relay.at[ring], r1.at[2 * k + 1])
        arrived(out.at[at], r1.at[2 * k])
        spread(k, zs, ys, out.at[at], relay.at[ring])
    for k, (dz, dy) in enumerate(((0, 0),) + ORDER):
        zs, ys = behind(z, dz), behind(y, dy)
        for j, d in ((1, 1), (2, 3), (0, 2)):
            at = slot(zs, behind(x, d), ys, c)
            arrived(out.at[at], r2.at[3 * k + j])
            send(out.at[at], out.at[at], s3.at[4 * k + 1 + j], r3.at[4 * k + 1 + j], device(z, x, y, 1 - c))
    for k, (dz, dy) in enumerate(((0, 0),) + ORDER):
        zs, ys = behind(z, dz), behind(y, dy)
        for j, d in ((-1, 0), (1, 1), (2, 3), (0, 2)):
            arrived(out.at[slot(zs, behind(x, d), ys, 1 - c)], r3.at[4 * k + 1 + j])
    for copy in sends:
        copy.wait_send()
    keep.wait()


def exchange(volts, window, dft, mask):
    dma = pltpu.SemaphoreType.DMA
    whole = pl.BlockSpec(memory_space=pltpu.VMEM)
    return pl.pallas_call(
        exchange_kernel,
        out_shape=jax.ShapeDtypeStruct((128, DEPTH, LOCAL, 2 * SPECTRA), jnp.bfloat16),
        in_specs=[whole] * 4,
        out_specs=pl.BlockSpec(memory_space=pl.ANY),
        scratch_shapes=[
            pltpu.VMEM((3, SPECTRA * LOCAL, 128), jnp.float32),
            pltpu.VMEM((2 * BAND * LOCAL, SPECTRA), jnp.float32),
            pltpu.VMEM((RINGS, 2, DEPTH, LOCAL, 2 * SPECTRA), jnp.bfloat16),
            pltpu.VMEM((RINGS, DEPTH, LOCAL, 2 * SPECTRA), jnp.bfloat16),
            dma((2 * RINGS,)),
            dma((2 * RINGS,)),
            dma((3 * RINGS,)),
            dma((3 * RINGS,)),
            dma((4 * RINGS,)),
            dma((4 * RINGS,)),
            dma,
        ],
        compiler_params=pltpu.CompilerParams(
            collective_id=0, has_side_effects=True, vmem_limit_bytes=32 * 1024 * 1024
        ),
        cost_estimate=pl.CostEstimate(flops=2 * 3 * 192 * 384 * 2048, bytes_accessed=6 << 20, transcendentals=1536),
        name="exchange",
    )(volts, window, dft, mask)


def correlate_kernel(rows, table, spectra, out):
    first = pl.program_id(1) * rows
    for r in range(rows):
        a, b = table[first + r, 0], table[first + r, 1]
        left = spectra[pl.ds(a * LOCAL, LOCAL), 0].reshape(BLOCK, 2 * SPECTRA)
        right = spectra[pl.ds(b * LOCAL, LOCAL), 0].reshape(BLOCK, 2 * SPECTRA)
        turned = jnp.concatenate([left[:, SPECTRA:], -left[:, :SPECTRA]], axis=1)
        for part, lhs in ((0, left), (1, turned)):
            vis = lax.dot_general(lhs, right, (((1,), (1,)), ((), ())), preferred_element_type=jnp.float32)
            out[r, 0, part] = (vis * (1.0 / SPECTRA)).astype(jnp.bfloat16)


def correlate(table, spectra):
    pairs, rows = table.shape[0], 3
    return pl.pallas_call(
        functools.partial(correlate_kernel, rows),
        out_shape=jax.ShapeDtypeStruct((pairs, DEPTH, 2, BLOCK, BLOCK), jnp.bfloat16),
        grid_spec=pltpu.PrefetchScalarGridSpec(
            num_scalar_prefetch=1,
            grid=(DEPTH, pairs // rows),
            in_specs=[pl.BlockSpec((128, 1, LOCAL, 2 * SPECTRA), lambda ch, p, table: (0, ch, 0, 0))],
            out_specs=pl.BlockSpec((rows, 1, 2, BLOCK, BLOCK), lambda ch, p, table: (p, ch, 0, 0, 0)),
        ),
        compiler_params=pltpu.CompilerParams(vmem_limit_bytes=32 * 1024 * 1024),
        cost_estimate=pl.CostEstimate(flops=2 * 54 * 256**3, bytes_accessed=10 << 20, transcendentals=0),
        name="correlate",
    )(table, spectra)


def body(voltages, input_alive_mask, pair_table):
    window, dft = tables()
    spectra = exchange(voltages, jnp.asarray(window), jnp.asarray(dft), input_alive_mask.reshape(LOCAL, 1))
    return correlate(pair_table, spectra)


def solution(mesh):
    in_specs = (P(("freq", "pair"), None), P(("freq", "pair")), P("pair", None))
    out_specs = P("pair", "freq", None, None, None)
    return jax.shard_map(body, mesh=mesh, in_specs=in_specs, out_specs=out_specs, check_vma=False)
```

```python
import math

import jax
import jax.numpy as jnp
import numpy as np
from jax import lax
from jax.experimental import pallas as pl
from jax.experimental.pallas import tpu as pltpu
from jax.sharding import PartitionSpec as P

CHAN = 192
BAND = 96
TAPS = 4
SPECTRA = 128
BLOCK = 256
PERIOD = 2 * CHAN
SIDE = 4
RINGS = SIDE * SIDE
LOCAL = 16
DEPTH = 3
GROUPS = BAND // DEPTH
MESH = pl.DeviceIdType.MESH

ORDER = (
    (1, 0), (0, 1), (3, 0), (0, 3), (2, 0), (0, 2), (1, 1), (3, 3),
    (1, 3), (3, 1), (2, 1), (1, 2), (2, 3), (3, 2), (2, 2),
)


def tables():
    length = TAPS * PERIOD
    j = np.arange(length, dtype=np.float64)
    window = np.sinc((j - length / 2 + 0.5) / PERIOD) * (0.54 - 0.46 * np.cos(2 * math.pi * j / (length - 1)))
    window = window.reshape(TAPS, PERIOD).astype(np.float32)
    z, y, q, ch = np.meshgrid(np.arange(4), np.arange(4), np.arange(2), np.arange(DEPTH), indexing="ij")
    k = ((z * 8 + q * 4 + y) * DEPTH + ch).reshape(-1)
    phase = 2 * math.pi / PERIOD * (k[:, None] * np.arange(PERIOD)[None, :] % PERIOD)
    rows = np.stack([np.cos(phase), -np.sin(phase)], axis=1).reshape(2 * BAND, PERIOD)
    high = rows.astype(jnp.bfloat16).astype(np.float64)
    low = (rows - high).astype(jnp.bfloat16)
    return np.concatenate([high, low.astype(np.float64), window, np.zeros((8 - TAPS, PERIOD))]).astype(np.float32)


def place():
    f, p = lax.axis_index("freq"), lax.axis_index("pair")
    z, x_lo, y = lax.div(f, 8), lax.rem(lax.div(f, 4), 2), lax.rem(f, 4)
    return z, lax.div(p, 2) * 2 + x_lo, y, lax.rem(p, 2)


def device(z, x, y, c):
    return (z * 8 + lax.rem(x, 2) * 4 + y, lax.div(x, 2) * 2 + c)


def slot(z, x, y, c):
    f, p = device(z, x, y, c)
    return f * 4 + p


def ahead(a, d):
    return lax.rem(a + d, SIDE)


def behind(a, d):
    return lax.rem(a + SIDE - d, SIDE)


CHUNKS = 4
STEP = SPECTRA // CHUNKS
PITCH = LOCAL + 8


def chunk(c):
    first = 0 if c == 0 else c * STEP + TAPS - 1
    return pl.ds(first * PERIOD, ((c + 1) * STEP + TAPS - 1 - first) * PERIOD)


def channelize(volts_hbm, table_hbm, mask, volts, table, dft, fir, spec, ready, load):
    loads = [pltpu.make_async_copy(table_hbm, table, load.at[CHUNKS])]
    for c in range(CHUNKS):
        loads.append(pltpu.make_async_copy(volts_hbm.at[:, chunk(c)], volts.at[:, chunk(c)], load.at[c]))
    loads[1].start()
    loads[0].start()
    for part in loads[2:]:
        part.start()
    loads[0].wait()
    rows = 2 * BAND
    dft[:, 0:PERIOD] = table[0:rows].astype(jnp.bfloat16)
    dft[:, PERIOD : 2 * PERIOD] = table[rows : 2 * rows].astype(jnp.bfloat16)
    dft[:, 2 * PERIOD :] = dft[:, 0:PERIOD]

    def filt(step, carry):
        first = step * 8
        frames = []
        for t in range(8 + TAPS - 1):
            at = pl.multiple_of((first + t) * PERIOD, 128)
            frames.append(volts[:, pl.ds(at, PERIOD)].astype(jnp.float32))
        window = [table[2 * rows + m : 2 * rows + m + 1, :] for m in range(TAPS)]
        for t in range(8):
            total = window[0] * frames[t]
            for m in range(1, TAPS):
                total = total + window[m] * frames[t + m]
            row = pl.multiple_of((first + t) * PITCH, 8)
            for j in range(3):
                fir[j, pl.ds(row, LOCAL), :] = total[:, j * 128 : (j + 1) * 128]
        return carry

    for c in range(CHUNKS):
        loads[1 + c].wait()
        lax.fori_loop(c * STEP // 8, (c + 1) * STEP // 8, filt, 0, unroll=True)

    for pair in range(LOCAL // 2):
        highs, lows = [], []
        for i in (2 * pair, 2 * pair + 1):
            x = jnp.concatenate([fir[j, pl.ds(i, SPECTRA, stride=PITCH), :] for j in range(3)], axis=1)
            high = x.astype(jnp.bfloat16)
            highs.append(high)
            lows.append((x - high.astype(jnp.float32)).astype(jnp.bfloat16))
        high, low = jnp.concatenate(highs, axis=0), jnp.concatenate(lows, axis=0)
        right = jnp.concatenate([high, high, low], axis=1)
        out = lax.dot_general(dft[...], right, (((1,), (1,)), ((), ())), preferred_element_type=jnp.float32)
        for half in range(2):
            spec[pl.ds(2 * pair + half, rows, stride=LOCAL), :] = out[:, half * SPECTRA : (half + 1) * SPECTRA]

    inputs = lax.broadcasted_iota(jnp.int32, (LOCAL, 1), 0)
    alive = jnp.zeros((LOCAL, 1), jnp.float32)
    for i in range(LOCAL):
        alive = jnp.where(inputs == i, mask[i].astype(jnp.float32), alive)

    def equalize(ring, carry):
        for e in range(2 * DEPTH):
            at = pl.multiple_of((ring * 2 * DEPTH + e) * 2 * LOCAL, 2 * LOCAL)
            re, im = spec[pl.ds(at, LOCAL), :], spec[pl.ds(at + LOCAL, LOCAL), :]
            power = jnp.sum(re * re + im * im, axis=1, keepdims=True) * (1.0 / SPECTRA)
            gain = lax.rsqrt(power + 1e-06) * alive
            both = jnp.concatenate([re * gain, im * gain], axis=1)
            ready[ring, e // DEPTH, e % DEPTH] = both.astype(jnp.bfloat16)
        return carry

    lax.fori_loop(0, RINGS, equalize, 0, unroll=4)


def exchange_kernel(
    volts_hbm, table_hbm, mask, out, volts, table, dft, fir, spec, ready, relay, load, s1, r1, s2, r2, s3, r3, sl
):
    z, x, y, c = place()
    q = lax.rem(x, 2)
    barrier = pltpu.get_barrier_semaphore()
    peers = [device(ahead(z, dz), x, ahead(y, dy), c) for dz, dy in ORDER]
    peers += [device(z, ahead(x, d), y, c) for d in (1, 2, 3)] + [device(z, x, y, 1 - c)]
    for peer in peers:
        pl.semaphore_signal(barrier, inc=1, device_id=peer, device_id_type=MESH)

    channelize(volts_hbm, table_hbm, mask, volts, table, dft, fir, spec, ready, load)

    pl.semaphore_wait(barrier, len(peers))
    sends = []

    def send(src, dst, send_sem, recv_sem, to):
        copy = pltpu.make_async_remote_copy(
            src_ref=src, dst_ref=dst, send_sem=send_sem, recv_sem=recv_sem, device_id=to, device_id_type=MESH
        )
        copy.start()
        sends.append(copy)

    def arrived(dst, sem):
        pltpu.make_async_copy(dst, dst, sem).wait()

    def spread(k, zs, ys, mine, others):
        at = slot(zs, x, ys, c)
        send(others, out.at[at], s2.at[3 * k + 1], r2.at[3 * k + 1], device(z, ahead(x, 1), y, c))
        send(others, out.at[at], s2.at[3 * k + 2], r2.at[3 * k + 2], device(z, ahead(x, 3), y, c))
        send(mine, out.at[at], s2.at[3 * k], r2.at[3 * k], device(z, ahead(x, 2), y, c))
        send(mine, out.at[at], s3.at[4 * k], r3.at[4 * k], device(z, x, y, 1 - c))

    here, own = z * SIDE + y, slot(z, x, y, c)
    spread(0, z, y, ready.at[here, q], ready.at[here, 1 - q])
    keep = pltpu.make_async_copy(ready.at[here, q], out.at[own], sl)
    keep.start()
    for k, (dz, dy) in enumerate(ORDER, 1):
        zd, yd = ahead(z, dz), ahead(y, dy)
        to, there = device(zd, x, yd, c), zd * SIDE + yd
        send(ready.at[there, 1 - q], relay.at[here], s1.at[2 * k + 1], r1.at[2 * k + 1], to)
        send(ready.at[there, q], out.at[own], s1.at[2 * k], r1.at[2 * k], to)
    for k, (dz, dy) in enumerate(ORDER, 1):
        zs, ys = behind(z, dz), behind(y, dy)
        at, ring = slot(zs, x, ys, c), zs * SIDE + ys
        arrived(relay.at[ring], r1.at[2 * k + 1])
        arrived(out.at[at], r1.at[2 * k])
        spread(k, zs, ys, out.at[at], relay.at[ring])
    for k, (dz, dy) in enumerate(((0, 0),) + ORDER):
        zs, ys = behind(z, dz), behind(y, dy)
        for j, d in ((1, 1), (2, 3), (0, 2)):
            at = slot(zs, behind(x, d), ys, c)
            arrived(out.at[at], r2.at[3 * k + j])
            send(out.at[at], out.at[at], s3.at[4 * k + 1 + j], r3.at[4 * k + 1 + j], device(z, x, y, 1 - c))
    for k, (dz, dy) in enumerate(((0, 0),) + ORDER):
        zs, ys = behind(z, dz), behind(y, dy)
        for j, d in ((-1, 0), (1, 1), (2, 3), (0, 2)):
            arrived(out.at[slot(zs, behind(x, d), ys, 1 - c)], r3.at[4 * k + 1 + j])
    for copy in sends:
        copy.wait_send()
    keep.wait()


def exchange(volts, table, mask):
    dma = pltpu.SemaphoreType.DMA
    anywhere = pl.BlockSpec(memory_space=pltpu.HBM)
    return pl.pallas_call(
        exchange_kernel,
        out_shape=pltpu.VMEM((128, DEPTH, LOCAL, 2 * SPECTRA), jnp.bfloat16),
        in_specs=[anywhere, anywhere, pl.BlockSpec(memory_space=pltpu.SMEM)],
        out_specs=pl.BlockSpec(memory_space=pl.ANY),
        scratch_shapes=[
            pltpu.VMEM(volts.shape, jnp.bfloat16),
            pltpu.VMEM(table.shape, jnp.float32),
            pltpu.VMEM((2 * BAND, 3 * PERIOD), jnp.bfloat16),
            pltpu.VMEM((3, SPECTRA * PITCH, 128), jnp.float32),
            pltpu.VMEM((2 * BAND * LOCAL, SPECTRA), jnp.float32),
            pltpu.VMEM((RINGS, 2, DEPTH, LOCAL, 2 * SPECTRA), jnp.bfloat16),
            pltpu.VMEM((RINGS, DEPTH, LOCAL, 2 * SPECTRA), jnp.bfloat16),
            dma((CHUNKS + 1,)),
            dma((2 * RINGS,)),
            dma((2 * RINGS,)),
            dma((3 * RINGS,)),
            dma((3 * RINGS,)),
            dma((4 * RINGS,)),
            dma((4 * RINGS,)),
            dma,
        ],
        compiler_params=pltpu.CompilerParams(
            collective_id=0, has_side_effects=True, vmem_limit_bytes=56 * 1024 * 1024
        ),
        cost_estimate=pl.CostEstimate(flops=2 * 3 * 192 * 384 * 2048, bytes_accessed=6 << 20, transcendentals=1536),
        name="exchange",
    )(volts, table, mask)


def correlate_kernel(table, spectra, out, vis, sem):
    pairs = out.shape[0]

    def pair(row, carry):
        a, b = table[0, row], table[1, row]
        for ch in range(DEPTH):
            left = spectra[pl.ds(a * LOCAL, LOCAL), ch].reshape(BLOCK, 2 * SPECTRA)
            right = spectra[pl.ds(b * LOCAL, LOCAL), ch].reshape(BLOCK, 2 * SPECTRA)
            turned = jnp.concatenate([left[:, SPECTRA:], -left[:, :SPECTRA]], axis=1)
            both = jnp.concatenate([left, turned], axis=0)
            sums = lax.dot_general(both, right, (((1,), (1,)), ((), ())), preferred_element_type=jnp.float32)
            vis[row, ch] = (sums * (1.0 / SPECTRA)).astype(jnp.bfloat16).reshape(2, BLOCK, BLOCK)
        pltpu.make_async_copy(vis.at[row], out.at[row], sem).start()
        return carry

    lax.fori_loop(0, pairs, pair, 0, unroll=3)
    pltpu.make_async_copy(vis, out, sem).wait()


def correlate(table, spectra):
    shape = (table.shape[1], DEPTH, 2, BLOCK, BLOCK)
    return pl.pallas_call(
        correlate_kernel,
        out_shape=jax.ShapeDtypeStruct(shape, jnp.bfloat16),
        in_specs=[pl.BlockSpec(memory_space=pltpu.SMEM), pl.BlockSpec(memory_space=pltpu.VMEM)],
        out_specs=pl.BlockSpec(memory_space=pl.ANY),
        scratch_shapes=[pltpu.VMEM(shape, jnp.bfloat16), pltpu.SemaphoreType.DMA],
        compiler_params=pltpu.CompilerParams(vmem_limit_bytes=32 * 1024 * 1024),
        cost_estimate=pl.CostEstimate(flops=2 * 54 * 256**3, bytes_accessed=10 << 20, transcendentals=0),
        name="correlate",
    )(table, spectra)


def body(voltages, input_alive_mask, pair_table):
    spectra = exchange(voltages, jnp.asarray(tables()), input_alive_mask)
    return correlate(pair_table.T, spectra)


def solution(mesh):
    in_specs = (P(("freq", "pair"), None), P(("freq", "pair")), P("pair", None))
    out_specs = P("pair", "freq", None, None, None)
    return jax.shard_map(body, mesh=mesh, in_specs=in_specs, out_specs=out_specs, check_vma=False)
```

```python
import math

import jax
import jax.numpy as jnp
import numpy as np
from jax import lax
from jax.experimental import pallas as pl
from jax.experimental.pallas import tpu as pltpu
from jax.sharding import PartitionSpec as P

CHAN = 192
BAND = 96
TAPS = 4
SPECTRA = 128
BLOCK = 256
PERIOD = 2 * CHAN
SIDE = 4
RINGS = SIDE * SIDE
LOCAL = 16
DEPTH = 3
GROUPS = BAND // DEPTH
MESH = pl.DeviceIdType.MESH

ORDER = ((0, 0), (0, 1), (0, 3), (1, 0), (1, 1), (1, 3), (0, 2), (1, 2))
HALF = len(ORDER)


def tables():
    length = TAPS * PERIOD
    j = np.arange(length, dtype=np.float64)
    window = np.sinc((j - length / 2 + 0.5) / PERIOD) * (0.54 - 0.46 * np.cos(2 * math.pi * j / (length - 1)))
    window = window.reshape(TAPS, PERIOD).astype(np.float32)
    z, y, q, ch = np.meshgrid(np.arange(4), np.arange(4), np.arange(2), np.arange(DEPTH), indexing="ij")
    k = ((z * 8 + q * 4 + y) * DEPTH + ch).reshape(-1)
    phase = 2 * math.pi / PERIOD * (k[:, None] * np.arange(PERIOD)[None, :] % PERIOD)
    rows = np.stack([np.cos(phase), -np.sin(phase)], axis=1).reshape(2 * BAND, PERIOD)
    high = rows.astype(jnp.bfloat16).astype(np.float64)
    low = (rows - high).astype(jnp.bfloat16)
    return np.concatenate([high, low.astype(np.float64), window, np.zeros((8 - TAPS, PERIOD))]).astype(np.float32)


def place():
    f, p = lax.axis_index("freq"), lax.axis_index("pair")
    z, x_lo, y = lax.div(f, 8), lax.rem(lax.div(f, 4), 2), lax.rem(f, 4)
    return z, lax.div(p, 2) * 2 + x_lo, y, lax.rem(p, 2)


def device(z, x, y, c):
    return (z * 8 + lax.rem(x, 2) * 4 + y, lax.div(x, 2) * 2 + c)


def slot(z, x, y, c):
    f, p = device(z, x, y, c)
    return f * 4 + p


def ahead(a, d):
    return lax.rem(a + d, SIDE)


def behind(a, d):
    return lax.rem(a + SIDE - d, SIDE)


CHUNKS = 4
STEP = SPECTRA // CHUNKS
PITCH = LOCAL + 8


def chunk(c):
    first = 0 if c == 0 else c * STEP + TAPS - 1
    return pl.ds(first * PERIOD, ((c + 1) * STEP + TAPS - 1 - first) * PERIOD)


def channelize(volts_hbm, table_hbm, volts, table, dft, fir, spec, load, greet):
    loads = [pltpu.make_async_copy(table_hbm, table, load.at[CHUNKS])]
    for c in range(CHUNKS):
        loads.append(pltpu.make_async_copy(volts_hbm.at[:, chunk(c)], volts.at[:, chunk(c)], load.at[c]))
    loads[1].start()
    loads[0].start()
    for part in loads[2:]:
        part.start()
    loads[0].wait()
    rows = 2 * BAND
    dft[:, 0:PERIOD] = table[0:rows].astype(jnp.bfloat16)
    dft[:, PERIOD : 2 * PERIOD] = table[rows : 2 * rows].astype(jnp.bfloat16)
    dft[:, 2 * PERIOD :] = dft[:, 0:PERIOD]

    def filt(step, carry):
        first = step * 8
        frames = []
        for t in range(8 + TAPS - 1):
            at = pl.multiple_of((first + t) * PERIOD, 128)
            frames.append(volts[:, pl.ds(at, PERIOD)].astype(jnp.float32))
        window = [table[2 * rows + m : 2 * rows + m + 1, :] for m in range(TAPS)]
        for t in range(8):
            total = window[0] * frames[t]
            for m in range(1, TAPS):
                total = total + window[m] * frames[t + m]
            row = pl.multiple_of((first + t) * PITCH, 8)
            for j in range(3):
                fir[j, pl.ds(row, LOCAL), :] = total[:, j * 128 : (j + 1) * 128]
        return carry

    for c in range(CHUNKS):
        loads[1 + c].wait()
        lax.fori_loop(c * STEP // 8, (c + 1) * STEP // 8, filt, 0, unroll=True)

    greet(1)

    for pair in range(LOCAL // 2):
        highs, lows = [], []
        for i in (2 * pair, 2 * pair + 1):
            x = jnp.concatenate([fir[j, pl.ds(i, SPECTRA, stride=PITCH), :] for j in range(3)], axis=1)
            high = x.astype(jnp.bfloat16)
            highs.append(high)
            lows.append((x - high.astype(jnp.float32)).astype(jnp.bfloat16))
        high, low = jnp.concatenate(highs, axis=0), jnp.concatenate(lows, axis=0)
        right = jnp.concatenate([high, high, low], axis=1)
        out = lax.dot_general(dft[...], right, (((1,), (1,)), ((), ())), preferred_element_type=jnp.float32)
        for half in range(2):
            spec[pl.ds(2 * pair + half, rows, stride=LOCAL), :] = out[:, half * SPECTRA : (half + 1) * SPECTRA]

    greet(0)


def equalize(ring, alive, spec, ready):
    for e in range(2 * DEPTH):
        at = pl.multiple_of((ring * 2 * DEPTH + e) * 2 * LOCAL, 2 * LOCAL)
        re, im = spec[pl.ds(at, LOCAL), :], spec[pl.ds(at + LOCAL, LOCAL), :]
        power = jnp.sum(re * re + im * im, axis=1, keepdims=True) * (1.0 / SPECTRA)
        gain = lax.rsqrt(power + 1e-06) * alive
        both = jnp.concatenate([re * gain, im * gain], axis=1)
        ready[ring, e // DEPTH, e % DEPTH] = both.astype(jnp.bfloat16)


def exchange_kernel(
    volts_hbm, table_hbm, mask, out, volts, table, dft, fir, spec, ready, relay, load, s1, r1, s2, r2, s3, r3, sl
):
    z, x, y, c = place()
    q, zc, zb = lax.rem(x, 2), lax.div(z, 2), lax.rem(z, 2)
    other_core = device(z, x, y, 1 - c)
    block = relay.at[0]
    barrier = pltpu.get_barrier_semaphore()

    def meet(f, j, sign):
        a, dy = ORDER[j]
        return lax.rem(zc + f, 2) * 2 + lax.rem(zb + a, 2), (ahead if sign > 0 else behind)(y, dy)

    def signal(to):
        pl.semaphore_signal(barrier, inc=1, device_id=to, device_id_type=MESH)

    for j in range(1, HALF):
        zd, yd = meet(0, j, 1)
        signal(device(zd, x, yd, c))
    for d in (1, 2, 3):
        signal(device(z, ahead(x, d), y, c))
    signal(other_core)

    def greet(part):
        @pl.when(zb == part)
        def _():
            pl.semaphore_wait(barrier, HALF + 3 + HALF * zc)
            for j in range(HALF):
                zd, yd = meet(1, j, 1)
                signal(device(zd, x, yd, c))

    channelize(volts_hbm, table_hbm, volts, table, dft, fir, spec, load, greet)
    inputs = lax.broadcasted_iota(jnp.int32, (LOCAL, 1), 0)
    alive = jnp.zeros((LOCAL, 1), jnp.float32)
    for i in range(LOCAL):
        alive = jnp.where(inputs == i, mask[i].astype(jnp.float32), alive)

    def send(src, dst, send_sem, recv_sem, to):
        pltpu.make_async_remote_copy(
            src_ref=src, dst_ref=dst, send_sem=send_sem, recv_sem=recv_sem, device_id=to, device_id_type=MESH
        ).start()

    def arrived(dst, sem):
        pltpu.make_async_copy(dst, dst, sem).wait()

    def spread(k, zs, ys, mine, others):
        at = slot(zs, x, ys, c)
        send(others, out.at[at], s2.at[3 * k + 1], r2.at[3 * k + 1], device(z, ahead(x, 1), y, c))
        send(others, out.at[at], s2.at[3 * k + 2], r2.at[3 * k + 2], device(z, ahead(x, 3), y, c))
        send(mine, out.at[at], s2.at[3 * k], r2.at[3 * k], device(z, ahead(x, 2), y, c))
        send(mine, out.at[at], s3.at[4 * k], r3.at[4 * k], other_core)

    here, own = z * SIDE + y, slot(z, x, y, c)

    def depart(f, j):
        k = f * HALF + j
        zd, yd = meet(f, j, 1)
        to, there = device(zd, x, yd, c), zd * SIDE + yd
        send(ready.at[there, 1 - q], relay.at[here], s1.at[2 * k + 1], r1.at[2 * k + 1], to)
        send(ready.at[there, q], out.at[own], s1.at[2 * k], r1.at[2 * k], to)

    def relay_on(f, j):
        k = f * HALF + j
        zs, ys = meet(f, j, -1)
        at, ring = slot(zs, x, ys, c), zs * SIDE + ys
        arrived(relay.at[ring], r1.at[2 * k + 1])
        arrived(out.at[at], r1.at[2 * k])
        spread(k, zs, ys, out.at[at], relay.at[ring])

    def hand_over(f, j):
        k = f * HALF + j
        zs, ys = meet(f, j, -1)
        for i, d in ((1, 1), (2, 3), (0, 2)):
            at = slot(zs, behind(x, d), ys, c)
            arrived(out.at[at], r2.at[3 * k + i])
            send(out.at[at], out.at[at], s3.at[4 * k + 1 + i], r3.at[4 * k + 1 + i], other_core)

    for j in range(HALF):
        zd, yd = meet(0, j, 1)
        equalize(zd * SIDE + yd, alive, spec, ready)
        if j == 0:
            spread(0, z, y, ready.at[here, q], ready.at[here, 1 - q])
            keep = pltpu.make_async_copy(ready.at[here, q], out.at[own], sl)
            keep.start()
        elif j == 3 or j == 7:
            for earlier in range(max(1, j - 3), j + 1):
                depart(0, earlier)
    for j in range(HALF):
        zd, yd = meet(1, j, 1)
        equalize(zd * SIDE + yd, alive, spec, ready)

    @pl.when(zc == 0)
    def _():
        for j in range(1, HALF):
            relay_on(0, j)
        pl.semaphore_wait(barrier, HALF)

    for j in range(HALF):
        depart(1, j)

    @pl.when(zc == 1)
    def _():
        for j in range(HALF):
            relay_on(1, j)

    for j in range(HALF):
        hand_over(zc, j)
        if j == 0:
            pl.when(zc == 0)(lambda: relay_on(1, 0))
        else:
            relay_on(1 - zc, j)
    for j in range(HALF):
        hand_over(1 - zc, j)

    def finish(sems, first, count):
        def one(i, carry):
            arrived(block, sems.at[i])
            return carry

        lax.fori_loop(first, count, one, 0)

    finish(r3, 0, 4 * RINGS)
    finish(s1, 2, 2 * RINGS)
    finish(s2, 0, 3 * RINGS)
    finish(s3, 0, 4 * RINGS)
    keep.wait()


def exchange(volts, table, mask):
    dma = pltpu.SemaphoreType.DMA
    anywhere = pl.BlockSpec(memory_space=pltpu.HBM)
    return pl.pallas_call(
        exchange_kernel,
        out_shape=pltpu.VMEM((128, DEPTH, LOCAL, 2 * SPECTRA), jnp.bfloat16),
        in_specs=[anywhere, anywhere, pl.BlockSpec(memory_space=pltpu.SMEM)],
        out_specs=pl.BlockSpec(memory_space=pl.ANY),
        scratch_shapes=[
            pltpu.VMEM(volts.shape, jnp.bfloat16),
            pltpu.VMEM(table.shape, jnp.float32),
            pltpu.VMEM((2 * BAND, 3 * PERIOD), jnp.bfloat16),
            pltpu.VMEM((3, SPECTRA * PITCH, 128), jnp.float32),
            pltpu.VMEM((2 * BAND * LOCAL, SPECTRA), jnp.float32),
            pltpu.VMEM((RINGS, 2, DEPTH, LOCAL, 2 * SPECTRA), jnp.bfloat16),
            pltpu.VMEM((RINGS, DEPTH, LOCAL, 2 * SPECTRA), jnp.bfloat16),
            dma((CHUNKS + 1,)),
            dma((2 * RINGS,)),
            dma((2 * RINGS,)),
            dma((3 * RINGS,)),
            dma((3 * RINGS,)),
            dma((4 * RINGS,)),
            dma((4 * RINGS,)),
            dma,
        ],
        compiler_params=pltpu.CompilerParams(
            collective_id=0, has_side_effects=True, vmem_limit_bytes=56 * 1024 * 1024
        ),
        cost_estimate=pl.CostEstimate(flops=2 * 3 * 192 * 384 * 2048, bytes_accessed=6 << 20, transcendentals=1536),
        name="exchange",
    )(volts, table, mask)


def correlate_kernel(table, spectra, out, vis, sem):
    pairs = out.shape[0]

    def pair(row, carry):
        a, b = table[0, row], table[1, row]
        for ch in range(DEPTH):
            left = spectra[pl.ds(a * LOCAL, LOCAL), ch].reshape(BLOCK, 2 * SPECTRA)
            right = spectra[pl.ds(b * LOCAL, LOCAL), ch].reshape(BLOCK, 2 * SPECTRA)
            turned = jnp.concatenate([left[:, SPECTRA:], -left[:, :SPECTRA]], axis=1)
            both = jnp.concatenate([left, turned], axis=0)
            sums = lax.dot_general(both, right, (((1,), (1,)), ((), ())), preferred_element_type=jnp.float32)
            vis[row, ch] = (sums * (1.0 / SPECTRA)).astype(jnp.bfloat16).reshape(2, BLOCK, BLOCK)
        pltpu.make_async_copy(vis.at[row], out.at[row], sem).start()
        return carry

    lax.fori_loop(0, pairs, pair, 0, unroll=3)
    pltpu.make_async_copy(vis, out, sem).wait()


def correlate(table, spectra):
    shape = (table.shape[1], DEPTH, 2, BLOCK, BLOCK)
    return pl.pallas_call(
        correlate_kernel,
        out_shape=jax.ShapeDtypeStruct(shape, jnp.bfloat16),
        in_specs=[pl.BlockSpec(memory_space=pltpu.SMEM), pl.BlockSpec(memory_space=pltpu.VMEM)],
        out_specs=pl.BlockSpec(memory_space=pl.ANY),
        scratch_shapes=[pltpu.VMEM(shape, jnp.bfloat16), pltpu.SemaphoreType.DMA],
        compiler_params=pltpu.CompilerParams(vmem_limit_bytes=32 * 1024 * 1024),
        cost_estimate=pl.CostEstimate(flops=2 * 54 * 256**3, bytes_accessed=10 << 20, transcendentals=0),
        name="correlate",
    )(table, spectra)


def body(voltages, input_alive_mask, pair_table):
    spectra = exchange(voltages, jnp.asarray(tables()), input_alive_mask)
    return correlate(pair_table.T, spectra)


def solution(mesh):
    in_specs = (P(("freq", "pair"), None), P(("freq", "pair")), P("pair", None))
    out_specs = P("pair", "freq", None, None, None)
    return jax.shard_map(body, mesh=mesh, in_specs=in_specs, out_specs=out_specs, check_vma=False)
```

```python
import math

import jax
import jax.numpy as jnp
import numpy as np
from jax import lax
from jax.experimental import pallas as pl
from jax.experimental.pallas import tpu as pltpu
from jax.sharding import PartitionSpec as P

CHAN = 192
BAND = 96
TAPS = 4
SPECTRA = 128
BLOCK = 256
PERIOD = 2 * CHAN
SIDE = 4
RINGS = SIDE * SIDE
LOCAL = 16
DEPTH = 3
GROUPS = BAND // DEPTH
MESH = pl.DeviceIdType.MESH

ORDER = (
    (0, 1), (3, 0), (0, 3), (3, 1), (0, 2), (3, 3), (2, 0), (3, 2),
    (2, 1), (1, 0), (2, 3), (1, 1), (2, 2), (1, 3), (1, 2),
)


PLANES = (0, 3, 2, 1)


def tables():
    length = TAPS * PERIOD
    j = np.arange(length, dtype=np.float64)
    window = np.sinc((j - length / 2 + 0.5) / PERIOD) * (0.54 - 0.46 * np.cos(2 * math.pi * j / (length - 1)))
    window = window.reshape(TAPS, PERIOD).astype(np.float32)
    z, y, q, ch = np.meshgrid(np.arange(4), np.arange(4), np.arange(2), np.arange(DEPTH), indexing="ij")
    k = ((z * 8 + q * 4 + y) * DEPTH + ch).reshape(-1)
    phase = 2 * math.pi / PERIOD * (k[:, None] * np.arange(PERIOD)[None, :] % PERIOD)
    rows = np.stack([np.cos(phase), -np.sin(phase)], axis=1).reshape(2 * BAND, PERIOD)
    high = rows.astype(jnp.bfloat16).astype(np.float64)
    low = (rows - high).astype(jnp.bfloat16)
    return np.concatenate([high, low.astype(np.float64), window, np.zeros((8 - TAPS, PERIOD))]).astype(np.float32)


def place():
    f, p = lax.axis_index("freq"), lax.axis_index("pair")
    z, x_lo, y = lax.div(f, 8), lax.rem(lax.div(f, 4), 2), lax.rem(f, 4)
    return z, lax.div(p, 2) * 2 + x_lo, y, lax.rem(p, 2)


def device(z, x, y, c):
    return (z * 8 + lax.rem(x, 2) * 4 + y, lax.div(x, 2) * 2 + c)


def slot(z, x, y, c):
    f, p = device(z, x, y, c)
    return f * 4 + p


def ahead(a, d):
    return lax.rem(a + d, SIDE)


def behind(a, d):
    return lax.rem(a + SIDE - d, SIDE)


CHUNKS = 4
STEP = SPECTRA // CHUNKS
PITCH = LOCAL + 8


def chunk(c):
    first = 0 if c == 0 else c * STEP + TAPS - 1
    return pl.ds(first * PERIOD, ((c + 1) * STEP + TAPS - 1 - first) * PERIOD)


def channelize(volts_hbm, table_hbm, volts, table, dft, fir, spec, load):
    loads = [pltpu.make_async_copy(table_hbm, table, load.at[CHUNKS])]
    for c in range(CHUNKS):
        loads.append(pltpu.make_async_copy(volts_hbm.at[:, chunk(c)], volts.at[:, chunk(c)], load.at[c]))
    loads[1].start()
    loads[0].start()
    for part in loads[2:]:
        part.start()
    loads[0].wait()
    rows = 2 * BAND
    dft[:, 0:PERIOD] = table[0:rows].astype(jnp.bfloat16)
    dft[:, PERIOD : 2 * PERIOD] = table[rows : 2 * rows].astype(jnp.bfloat16)
    dft[:, 2 * PERIOD :] = dft[:, 0:PERIOD]

    def filt(step, carry):
        first = step * 8
        frames = []
        for t in range(8 + TAPS - 1):
            at = pl.multiple_of((first + t) * PERIOD, 128)
            frames.append(volts[:, pl.ds(at, PERIOD)].astype(jnp.float32))
        window = [table[2 * rows + m : 2 * rows + m + 1, :] for m in range(TAPS)]
        for t in range(8):
            total = window[0] * frames[t]
            for m in range(1, TAPS):
                total = total + window[m] * frames[t + m]
            row = pl.multiple_of((first + t) * PITCH, 8)
            for j in range(3):
                fir[j, pl.ds(row, LOCAL), :] = total[:, j * 128 : (j + 1) * 128]
        return carry

    for c in range(CHUNKS):
        loads[1 + c].wait()
        lax.fori_loop(c * STEP // 8, (c + 1) * STEP // 8, filt, 0, unroll=True)

    for pair in range(LOCAL // 2):
        highs, lows = [], []
        for i in (2 * pair, 2 * pair + 1):
            x = jnp.concatenate([fir[j, pl.ds(i, SPECTRA, stride=PITCH), :] for j in range(3)], axis=1)
            high = x.astype(jnp.bfloat16)
            highs.append(high)
            lows.append((x - high.astype(jnp.float32)).astype(jnp.bfloat16))
        high, low = jnp.concatenate(highs, axis=0), jnp.concatenate(lows, axis=0)
        right = jnp.concatenate([high, high, low], axis=1)
        out = lax.dot_general(dft[...], right, (((1,), (1,)), ((), ())), preferred_element_type=jnp.float32)
        for half in range(2):
            spec[pl.ds(2 * pair + half, rows, stride=LOCAL), :] = out[:, half * SPECTRA : (half + 1) * SPECTRA]


def equalize(ring, alive, spec, ready):
    for e in range(2 * DEPTH):
        at = pl.multiple_of((ring * 2 * DEPTH + e) * 2 * LOCAL, 2 * LOCAL)
        re, im = spec[pl.ds(at, LOCAL), :], spec[pl.ds(at + LOCAL, LOCAL), :]
        power = jnp.sum(re * re + im * im, axis=1, keepdims=True) * (1.0 / SPECTRA)
        gain = lax.rsqrt(power + 1e-06) * alive
        both = jnp.concatenate([re * gain, im * gain], axis=1)
        ready[ring, e // DEPTH, e % DEPTH] = both.astype(jnp.bfloat16)


def exchange_kernel(
    volts_hbm, table_hbm, mask_hbm, out, volts, table, mask, dft, fir, spec, ready, relay, load, s1, s2, s3, r1, r2, r3, sl
):
    z, x, y, c = place()
    q = lax.rem(x, 2)
    here, own = z * SIDE + y, slot(z, x, y, c)
    other_core = device(z, x, y, 1 - c)
    barrier = pltpu.get_barrier_semaphore()
    peers = [device(ahead(z, dz), x, ahead(y, dy), c) for dz, dy in ORDER]
    peers += [device(z, ahead(x, d), y, c) for d in (1, 2, 3)] + [other_core]
    for peer in peers:
        pl.semaphore_signal(barrier, inc=1, device_id=peer, device_id_type=MESH)

    alive_load = pltpu.make_async_copy(mask_hbm, mask, load.at[CHUNKS + 1])
    alive_load.start()
    channelize(volts_hbm, table_hbm, volts, table, dft, fir, spec, load)
    alive_load.wait()
    inputs = lax.broadcasted_iota(jnp.int32, (LOCAL, 1), 0)
    alive = jnp.zeros((LOCAL, 1), jnp.float32)
    for i in range(LOCAL):
        alive = jnp.where(inputs == i, mask[i].astype(jnp.float32), alive)

    def send(src, dst, send_sem, recv_sem, to):
        pltpu.make_async_remote_copy(
            src_ref=src, dst_ref=dst, send_sem=send_sem, recv_sem=recv_sem, device_id=to, device_id_type=MESH
        ).start()

    def arrived(blocks, sem):
        pltpu.make_async_copy(blocks, blocks, sem).wait()

    def spread(ring, at, mine, others):
        send(others, out.at[at], s2, r2.at[ring], device(z, ahead(x, 1), y, c))
        send(others, out.at[at], s2, r2.at[ring], device(z, ahead(x, 3), y, c))
        send(mine, out.at[at], s2, r2.at[ring], device(z, ahead(x, 2), y, c))
        send(mine, out.at[at], s3, r3, other_core)

    def depart(dz, dy):
        zd, yd = ahead(z, dz), ahead(y, dy)
        to, there = device(zd, x, yd, c), zd * SIDE + yd
        send(ready.at[there, 1 - q], relay.at[here], s1, r1.at[here], to)
        send(ready.at[there, q], out.at[own], s1, r1.at[here], to)

    def relay_on(dz):
        zs = behind(z, dz)
        for dy in range(SIDE):
            ys = behind(y, dy)
            ring, at = zs * SIDE + ys, slot(zs, x, ys, c)
            if (dz, dy) != (0, 0):
                arrived(relay.at[pl.ds(0, 2)], r1.at[ring])
                spread(ring, at, out.at[at], relay.at[ring])

    def hand_over(dz):
        zs = behind(z, dz)
        for dy in range(SIDE):
            ys = behind(y, dy)
            arrived(relay.at[pl.ds(0, 3)], r2.at[zs * SIDE + ys])
            for d in (1, 3, 2):
                at = slot(zs, behind(x, d), ys, c)
                send(out.at[at], out.at[at], s3, r3, other_core)

    equalize(here, alive, spec, ready)
    pl.semaphore_wait(barrier, len(peers))
    spread(here, own, ready.at[here, q], ready.at[here, 1 - q])
    keep = pltpu.make_async_copy(ready.at[here, q], out.at[own], sl)
    keep.start()
    for first in range(0, len(ORDER), 3):
        for dz, dy in ORDER[first : first + 3]:
            equalize(ahead(z, dz) * SIDE + ahead(y, dy), alive, spec, ready)
        for dz, dy in ORDER[first : first + 3]:
            depart(dz, dy)
    relay_on(PLANES[0])
    for last, dz in zip(PLANES, PLANES[1:]):
        relay_on(dz)
    for dz in PLANES:
        hand_over(dz)
    arrived(out.at[pl.ds(0, 4 * RINGS)], r3)
    arrived(ready.at[pl.ds(0, RINGS - 1)], s1)
    arrived(out.at[pl.ds(0, 3 * RINGS)], s2)
    arrived(out.at[pl.ds(0, 4 * RINGS)], s3)
    keep.wait()


def exchange(volts, table, mask):
    dma = pltpu.SemaphoreType.DMA
    anywhere = pl.BlockSpec(memory_space=pltpu.HBM)
    return pl.pallas_call(
        exchange_kernel,
        out_shape=pltpu.VMEM((128, DEPTH, LOCAL, 2 * SPECTRA), jnp.bfloat16),
        in_specs=[anywhere] * 3,
        out_specs=pl.BlockSpec(memory_space=pl.ANY),
        scratch_shapes=[
            pltpu.VMEM(volts.shape, jnp.bfloat16),
            pltpu.VMEM(table.shape, jnp.float32),
            pltpu.SMEM(mask.shape, jnp.int32),
            pltpu.VMEM((2 * BAND, 3 * PERIOD), jnp.bfloat16),
            pltpu.VMEM((3, SPECTRA * PITCH, 128), jnp.float32),
            pltpu.VMEM((2 * BAND * LOCAL, SPECTRA), jnp.float32),
            pltpu.VMEM((RINGS, 2, DEPTH, LOCAL, 2 * SPECTRA), jnp.bfloat16),
            pltpu.VMEM((RINGS, DEPTH, LOCAL, 2 * SPECTRA), jnp.bfloat16),
            dma((CHUNKS + 2,)),
            dma,
            dma,
            dma,
            dma((RINGS,)),
            dma((RINGS,)),
            dma,
            dma,
        ],
        compiler_params=pltpu.CompilerParams(
            collective_id=0, has_side_effects=True, vmem_limit_bytes=56 * 1024 * 1024
        ),
        cost_estimate=pl.CostEstimate(flops=2 * 3 * 192 * 384 * 2048, bytes_accessed=6 << 20, transcendentals=1536),
        name="exchange",
    )(volts, table, mask)


def correlate_kernel(table, spectra, out, vis, sem):
    pairs = out.shape[0]

    def pair(row, carry):
        a, b = table[0, row], table[1, row]
        for ch in range(DEPTH):
            left = spectra[pl.ds(a * LOCAL, LOCAL), ch].reshape(BLOCK, 2 * SPECTRA)
            right = spectra[pl.ds(b * LOCAL, LOCAL), ch].reshape(BLOCK, 2 * SPECTRA)
            turned = jnp.concatenate([left[:, SPECTRA:], -left[:, :SPECTRA]], axis=1)
            both = jnp.concatenate([left, turned], axis=0)
            sums = lax.dot_general(both, right, (((1,), (1,)), ((), ())), preferred_element_type=jnp.float32)
            vis[row, ch] = (sums * (1.0 / SPECTRA)).astype(jnp.bfloat16).reshape(2, BLOCK, BLOCK)
        pltpu.make_async_copy(vis.at[row], out.at[row], sem).start()
        return carry

    lax.fori_loop(0, pairs, pair, 0, unroll=3)
    pltpu.make_async_copy(vis, out, sem).wait()


def correlate(table, spectra):
    shape = (table.shape[1], DEPTH, 2, BLOCK, BLOCK)
    return pl.pallas_call(
        correlate_kernel,
        out_shape=jax.ShapeDtypeStruct(shape, jnp.bfloat16),
        in_specs=[pl.BlockSpec(memory_space=pltpu.SMEM), pl.BlockSpec(memory_space=pltpu.VMEM)],
        out_specs=pl.BlockSpec(memory_space=pl.ANY),
        scratch_shapes=[pltpu.VMEM(shape, jnp.bfloat16), pltpu.SemaphoreType.DMA],
        compiler_params=pltpu.CompilerParams(vmem_limit_bytes=32 * 1024 * 1024),
        cost_estimate=pl.CostEstimate(flops=2 * 54 * 256**3, bytes_accessed=10 << 20, transcendentals=0),
        name="correlate",
    )(table, spectra)


def body(voltages, input_alive_mask, pair_table):
    spectra = exchange(voltages, jnp.asarray(tables()), input_alive_mask)
    return correlate(pair_table.T, spectra)


def solution(mesh):
    in_specs = (P(("freq", "pair"), None), P(("freq", "pair")), P("pair", None))
    out_specs = P("pair", "freq", None, None, None)
    return jax.shard_map(body, mesh=mesh, in_specs=in_specs, out_specs=out_specs, check_vma=False)
```

```python
import math

import jax
import jax.numpy as jnp
import numpy as np
from jax import lax
from jax.experimental import pallas as pl
from jax.experimental.pallas import tpu as pltpu
from jax.sharding import PartitionSpec as P

CHAN = 192
BAND = 96
TAPS = 4
SPECTRA = 128
BLOCK = 256
PERIOD = 2 * CHAN
SIDE = 4
RINGS = SIDE * SIDE
LOCAL = 16
DEPTH = 3
GROUPS = BAND // DEPTH
MESH = pl.DeviceIdType.MESH

NEAR = (1, 3, 2)


def tables():
    length = TAPS * PERIOD
    j = np.arange(length, dtype=np.float64)
    window = np.sinc((j - length / 2 + 0.5) / PERIOD) * (0.54 - 0.46 * np.cos(2 * math.pi * j / (length - 1)))
    window = window.reshape(TAPS, PERIOD).astype(np.float32)
    z, y, q, ch = np.meshgrid(np.arange(4), np.arange(4), np.arange(2), np.arange(DEPTH), indexing="ij")
    k = ((z * 8 + q * 4 + y) * DEPTH + ch).reshape(-1)
    phase = 2 * math.pi / PERIOD * (k[:, None] * np.arange(PERIOD)[None, :] % PERIOD)
    rows = np.stack([np.cos(phase), -np.sin(phase)], axis=1).reshape(2 * BAND, PERIOD)
    high = rows.astype(jnp.bfloat16).astype(np.float64)
    low = (rows - high).astype(jnp.bfloat16)
    return np.concatenate([high, low.astype(np.float64), window, np.zeros((8 - TAPS, PERIOD))]).astype(np.float32)


def place():
    f, p = lax.axis_index("freq"), lax.axis_index("pair")
    z, x_lo, y = lax.div(f, 8), lax.rem(lax.div(f, 4), 2), lax.rem(f, 4)
    return z, lax.div(p, 2) * 2 + x_lo, y, lax.rem(p, 2)


def device(z, x, y, c):
    return (z * 8 + lax.rem(x, 2) * 4 + y, lax.div(x, 2) * 2 + c)


def slot(z, x, y, c):
    f, p = device(z, x, y, c)
    return f * 4 + p


def ahead(a, d):
    return lax.rem(a + d, SIDE)


def behind(a, d):
    return lax.rem(a + SIDE - d, SIDE)


CHUNKS = 4
STEP = SPECTRA // CHUNKS
PITCH = LOCAL + 8


def chunk(c):
    first = 0 if c == 0 else c * STEP + TAPS - 1
    return pl.ds(first * PERIOD, ((c + 1) * STEP + TAPS - 1 - first) * PERIOD)


def channelize(volts_hbm, table_hbm, volts, table, dft, fir, spec, load, between):
    loads = [pltpu.make_async_copy(table_hbm, table, load.at[CHUNKS])]
    for c in range(CHUNKS):
        loads.append(pltpu.make_async_copy(volts_hbm.at[:, chunk(c)], volts.at[:, chunk(c)], load.at[c]))
    loads[1].start()
    loads[0].start()
    for part in loads[2:]:
        part.start()
    loads[0].wait()
    rows = 2 * BAND
    parts = table[0 : 2 * rows].astype(jnp.bfloat16)
    dft[:, 0:PERIOD] = parts
    dft[:, PERIOD:] = parts

    def filt(step, carry):
        first = step * 8
        frames = []
        for t in range(8 + TAPS - 1):
            at = pl.multiple_of((first + t) * PERIOD, 128)
            frames.append(volts[:, pl.ds(at, PERIOD)].astype(jnp.float32))
        window = [table[2 * rows + m : 2 * rows + m + 1, :] for m in range(TAPS)]
        for t in range(8):
            total = window[0] * frames[t]
            for m in range(1, TAPS):
                total = total + window[m] * frames[t + m]
            row = pl.multiple_of((first + t) * PITCH, 8)
            for j in range(3):
                fir[j, pl.ds(row, LOCAL), :] = total[:, j * 128 : (j + 1) * 128]
        return carry

    for c in range(CHUNKS):
        loads[1 + c].wait()
        lax.fori_loop(c * STEP // 8, (c + 1) * STEP // 8, filt, 0, unroll=True)

    between()
    for pair in range(LOCAL // 2):
        highs, lows = [], []
        for i in (2 * pair, 2 * pair + 1):
            x = jnp.concatenate([fir[j, pl.ds(i, SPECTRA, stride=PITCH), :] for j in range(3)], axis=1)
            high = x.astype(jnp.bfloat16)
            highs.append(high)
            lows.append((x - high.astype(jnp.float32)).astype(jnp.bfloat16))
        high, low = jnp.concatenate(highs, axis=0), jnp.concatenate(lows, axis=0)
        right = jnp.concatenate([high, low], axis=1)
        both = lax.dot_general(dft[...], right, (((1,), (1,)), ((), ())), preferred_element_type=jnp.float32)
        out = both[:rows] + both[rows:]
        for half in range(2):
            spec[pl.ds(2 * pair + half, rows, stride=LOCAL), :] = out[:, half * SPECTRA : (half + 1) * SPECTRA]


def equalize(ring, alive, spec, ready):
    for e in range(2 * DEPTH):
        at = pl.multiple_of((ring * 2 * DEPTH + e) * 2 * LOCAL, 2 * LOCAL)
        re, im = spec[pl.ds(at, LOCAL), :], spec[pl.ds(at + LOCAL, LOCAL), :]
        power = jnp.sum(re * re + im * im, axis=1, keepdims=True) * (1.0 / SPECTRA)
        gain = lax.rsqrt(power + 1e-06) * alive
        both = jnp.concatenate([re * gain, im * gain], axis=1)
        ready[ring, e // DEPTH, e % DEPTH] = both.astype(jnp.bfloat16)


def exchange_kernel(
    volts_hbm, table_hbm, mask_hbm, pairs_hbm, out, pairs, volts, table, mask, dft, fir, spec, ready, relay, load, s1, s2, s3, r1, r2, r3, sl
):
    z, x, y, c = place()
    q = lax.rem(x, 2)
    here, own = z * SIDE + y, slot(z, x, y, c)
    other_core = device(z, x, y, 1 - c)
    barrier = pltpu.get_barrier_semaphore()

    def signal(to):
        pl.semaphore_signal(barrier, inc=1, device_id=to, device_id_type=MESH)

    def plane(zd):
        for dy in range(SIDE):
            signal(device(zd, x, ahead(y, dy), c))

    for dy in NEAR:
        signal(device(z, x, ahead(y, dy), c))
    for d in (1, 2, 3):
        signal(device(z, ahead(x, d), y, c))
    signal(other_core)
    for dz in (1, 2, 3):
        pl.when((z > 0) & (ahead(z, dz) > 0))(lambda dz=dz: plane(ahead(z, dz)))

    def greet_first():
        pl.semaphore_wait(barrier, 7)
        for zd in (1, 2, 3):
            plane(zd)

    def greet_others():
        pl.semaphore_wait(barrier, 7 + 3 * SIDE)
        plane(0)

    def between():
        pl.when(z == 0)(greet_first)
        pl.when(z == 3)(greet_others)

    alive_load = pltpu.make_async_copy(mask_hbm, mask, load.at[CHUNKS + 1])
    alive_load.start()
    pairs_load = pltpu.make_async_copy(pairs_hbm, pairs, load.at[CHUNKS + 2])
    pairs_load.start()
    channelize(volts_hbm, table_hbm, volts, table, dft, fir, spec, load, between)
    pl.when((z == 1) | (z == 2))(greet_others)
    alive_load.wait()
    inputs = lax.broadcasted_iota(jnp.int32, (LOCAL, 1), 0)
    alive = jnp.zeros((LOCAL, 1), jnp.float32)
    for i in range(LOCAL):
        alive = jnp.where(inputs == i, mask[i].astype(jnp.float32), alive)

    def send(src, dst, send_sem, recv_sem, to):
        pltpu.make_async_remote_copy(
            src_ref=src, dst_ref=dst, send_sem=send_sem, recv_sem=recv_sem, device_id=to, device_id_type=MESH
        ).start()

    def arrived(blocks, sem):
        pltpu.make_async_copy(blocks, blocks, sem).wait()

    def spread(ring, at, mine, others):
        send(others, out.at[at], s2, r2.at[ring], device(z, ahead(x, 1), y, c))
        send(others, out.at[at], s2, r2.at[ring], device(z, ahead(x, 3), y, c))
        send(mine, out.at[at], s2, r2.at[ring], device(z, ahead(x, 2), y, c))
        send(mine, out.at[at], s3, r3, other_core)

    def prepare(dz):
        for dy in ((0,) if dz else ()) + NEAR:
            equalize(ahead(z, dz) * SIDE + ahead(y, dy), alive, spec, ready)

    def depart(zd, offsets=(0,) + NEAR):
        for dy in offsets:
            yd = ahead(y, dy)
            to, there = device(zd, x, yd, c), zd * SIDE + yd
            send(ready.at[there, 1 - q], relay.at[here], s1, r1.at[here], to)
            send(ready.at[there, q], out.at[own], s1, r1.at[here], to)

    def relay_on(zs, offsets=(0,) + NEAR):
        for dy in offsets:
            ys = behind(y, dy)
            ring, at = zs * SIDE + ys, slot(zs, x, ys, c)
            arrived(relay.at[pl.ds(0, 2)], r1.at[ring])
            spread(ring, at, out.at[at], relay.at[ring])

    def hand_over(zs):
        for dy in (0,) + NEAR:
            ys = behind(y, dy)
            arrived(relay.at[pl.ds(0, 3)], r2.at[zs * SIDE + ys])
            for d in (1, 3, 2):
                at = slot(zs, behind(x, d), ys, c)
                send(out.at[at], out.at[at], s3, r3, other_core)

    equalize(here, alive, spec, ready)
    spread(here, own, ready.at[here, q], ready.at[here, 1 - q])
    keep = pltpu.make_async_copy(ready.at[here, q], out.at[own], sl)
    keep.start()
    late = lax.div(z, 3)
    order = [behind(z, dz) for dz in (3 - late, 2 - late, 1 + 2 * late)]
    prepare(0)
    depart(z, NEAR)
    for dz in (3, 2, 1):
        prepare(dz)

    @pl.when(z > 0)
    def _():
        for dz in (3, 2, 1):
            depart(ahead(z, dz))

    relay_on(z, NEAR)

    @pl.when(z == 0)
    def _():
        pl.semaphore_wait(barrier, 3 * SIDE)
        for zd in (3, 2, 1):
            depart(zd)

    for zs in order:
        relay_on(zs)
    for zs in [z] + order:
        hand_over(zs)
    arrived(out.at[pl.ds(0, 4 * RINGS)], r3)
    arrived(ready.at[pl.ds(0, RINGS - 1)], s1)
    arrived(out.at[pl.ds(0, 3 * RINGS)], s2)
    arrived(out.at[pl.ds(0, 4 * RINGS)], s3)
    keep.wait()
    pairs_load.wait()


def exchange(volts, table, mask, pairs):
    dma = pltpu.SemaphoreType.DMA
    anywhere = pl.BlockSpec(memory_space=pltpu.HBM)
    return pl.pallas_call(
        exchange_kernel,
        out_shape=(
            pltpu.VMEM((128, DEPTH, LOCAL, 2 * SPECTRA), jnp.bfloat16),
            pltpu.SMEM(pairs.shape, pairs.dtype),
        ),
        in_specs=[anywhere] * 4,
        out_specs=(pl.BlockSpec(memory_space=pl.ANY), pl.BlockSpec(memory_space=pl.ANY)),
        scratch_shapes=[
            pltpu.VMEM(volts.shape, jnp.bfloat16),
            pltpu.VMEM(table.shape, jnp.float32),
            pltpu.SMEM(mask.shape, jnp.int32),
            pltpu.VMEM((4 * BAND, 2 * PERIOD), jnp.bfloat16),
            pltpu.VMEM((3, SPECTRA * PITCH, 128), jnp.float32),
            pltpu.VMEM((2 * BAND * LOCAL, SPECTRA), jnp.float32),
            pltpu.VMEM((RINGS, 2, DEPTH, LOCAL, 2 * SPECTRA), jnp.bfloat16),
            pltpu.VMEM((RINGS, DEPTH, LOCAL, 2 * SPECTRA), jnp.bfloat16),
            dma((CHUNKS + 3,)),
            dma,
            dma,
            dma,
            dma((RINGS,)),
            dma((RINGS,)),
            dma,
            dma,
        ],
        compiler_params=pltpu.CompilerParams(
            collective_id=0, has_side_effects=True, vmem_limit_bytes=56 * 1024 * 1024
        ),
        cost_estimate=pl.CostEstimate(flops=2 * 3 * 192 * 384 * 2048, bytes_accessed=6 << 20, transcendentals=1536),
        name="exchange",
    )(volts, table, mask, pairs)


def correlate_kernel(table, spectra, out, vis, sem):
    pairs = out.shape[0]

    def pair(row, carry):
        a, b = table[0, row], table[1, row]
        for ch in range(DEPTH):
            left = spectra[pl.ds(a * LOCAL, LOCAL), ch].reshape(BLOCK, 2 * SPECTRA)
            right = spectra[pl.ds(b * LOCAL, LOCAL), ch].reshape(BLOCK, 2 * SPECTRA)
            turned = jnp.concatenate([left[:, SPECTRA:], -left[:, :SPECTRA]], axis=1)
            both = jnp.concatenate([left, turned], axis=0)
            sums = lax.dot_general(both, right, (((1,), (1,)), ((), ())), preferred_element_type=jnp.float32)
            vis[row, ch] = (sums * (1.0 / SPECTRA)).astype(jnp.bfloat16).reshape(2, BLOCK, BLOCK)
            pltpu.make_async_copy(vis.at[row, ch], out.at[row, ch], sem).start()
        return carry

    lax.fori_loop(0, pairs, pair, 0, unroll=True)
    pltpu.make_async_copy(vis, out, sem).wait()


def correlate(table, spectra):
    shape = (table.shape[1], DEPTH, 2, BLOCK, BLOCK)
    return pl.pallas_call(
        correlate_kernel,
        out_shape=jax.ShapeDtypeStruct(shape, jnp.bfloat16),
        in_specs=[pl.BlockSpec(memory_space=pltpu.SMEM), pl.BlockSpec(memory_space=pltpu.VMEM)],
        out_specs=pl.BlockSpec(memory_space=pl.ANY),
        scratch_shapes=[pltpu.VMEM(shape, jnp.bfloat16), pltpu.SemaphoreType.DMA],
        compiler_params=pltpu.CompilerParams(vmem_limit_bytes=32 * 1024 * 1024),
        cost_estimate=pl.CostEstimate(flops=2 * 54 * 256**3, bytes_accessed=10 << 20, transcendentals=0),
        name="correlate",
    )(table, spectra)


def body(voltages, input_alive_mask, pair_table):
    spectra, pairs = exchange(voltages, jnp.asarray(tables()), input_alive_mask, pair_table.T)
    return correlate(pairs, spectra)


def solution(mesh):
    in_specs = (P(("freq", "pair"), None), P(("freq", "pair")), P("pair", None))
    out_specs = P("pair", "freq", None, None, None)
    return jax.shard_map(body, mesh=mesh, in_specs=in_specs, out_specs=out_specs, check_vma=False)
```

```python
import math

import jax
import jax.numpy as jnp
import numpy as np
from jax import lax
from jax.experimental import pallas as pl
from jax.experimental.pallas import tpu as pltpu
from jax.sharding import PartitionSpec as P

CHAN = 192
BAND = 96
TAPS = 4
SPECTRA = 128
BLOCK = 256
PERIOD = 2 * CHAN
SIDE = 4
RINGS = SIDE * SIDE
LOCAL = 16
DEPTH = 3
GROUPS = BAND // DEPTH
MESH = pl.DeviceIdType.MESH

NEAR = (1, 3, 2)


def tables():
    length = TAPS * PERIOD
    j = np.arange(length, dtype=np.float64)
    window = np.sinc((j - length / 2 + 0.5) / PERIOD) * (0.54 - 0.46 * np.cos(2 * math.pi * j / (length - 1)))
    window = window.reshape(TAPS, PERIOD).astype(np.float32)
    z, y, q, ch = np.meshgrid(np.arange(4), np.arange(4), np.arange(2), np.arange(DEPTH), indexing="ij")
    k = ((z * 8 + q * 4 + y) * DEPTH + ch).reshape(-1)
    phase = 2 * math.pi / PERIOD * (k[:, None] * np.arange(PERIOD)[None, :] % PERIOD)
    rows = np.stack([np.cos(phase), -np.sin(phase)], axis=1).reshape(2 * BAND, PERIOD)
    high = rows.astype(jnp.bfloat16).astype(np.float64)
    low = (rows - high).astype(jnp.bfloat16)
    return np.concatenate([high, low.astype(np.float64), window, np.zeros((8 - TAPS, PERIOD))]).astype(np.float32)


def place():
    f, p = lax.axis_index("freq"), lax.axis_index("pair")
    z, x_lo, y = lax.div(f, 8), lax.rem(lax.div(f, 4), 2), lax.rem(f, 4)
    return z, lax.div(p, 2) * 2 + x_lo, y, lax.rem(p, 2)


def device(z, x, y, c):
    return (z * 8 + lax.rem(x, 2) * 4 + y, lax.div(x, 2) * 2 + c)


def slot(z, x, y, c):
    f, p = device(z, x, y, c)
    return f * 4 + p


def ahead(a, d):
    return lax.rem(a + d, SIDE)


def behind(a, d):
    return lax.rem(a + SIDE - d, SIDE)


CHUNKS = 4
STEP = SPECTRA // CHUNKS
PITCH = LOCAL + 1


def chunk(c):
    first = 0 if c == 0 else c * STEP + TAPS - 1
    return pl.ds(first * PERIOD, ((c + 1) * STEP + TAPS - 1 - first) * PERIOD)


def channelize(volts_hbm, table_hbm, volts, table, dft, fir, spec, load, between):
    rows = 2 * BAND
    loads = []
    for c in range(CHUNKS):
        loads.append(pltpu.make_async_copy(volts_hbm.at[:, chunk(c)], volts.at[:, chunk(c)], load.at[c]))
    taps = pltpu.make_async_copy(table_hbm.at[pl.ds(2 * rows, 8)], table.at[pl.ds(2 * rows, 8)], load.at[CHUNKS + 3])
    waves = pltpu.make_async_copy(table_hbm.at[pl.ds(0, 2 * rows)], table.at[pl.ds(0, 2 * rows)], load.at[CHUNKS])
    taps.start()
    loads[0].start()
    loads[1].start()
    waves.start()
    for part in loads[2:]:
        part.start()
    taps.wait()

    def filt(step, carry):
        first = step * 8
        frames = []
        for t in range(8 + TAPS - 1):
            at = pl.multiple_of((first + t) * PERIOD, 128)
            frames.append(volts[:, pl.ds(at, PERIOD)].astype(jnp.float32))
        window = [table[2 * rows + m : 2 * rows + m + 1, :] for m in range(TAPS)]
        for t in range(8):
            total = window[0] * frames[t]
            for m in range(1, TAPS):
                total = total + window[m] * frames[t + m]
            row = (first + t) * PITCH
            for j in range(3):
                fir[j, pl.ds(row, LOCAL), :] = total[:, j * 128 : (j + 1) * 128]
        return carry

    for c in range(CHUNKS):
        loads[c].wait()
        if c == CHUNKS - 1:
            waves.wait()
            parts = table[0 : 2 * rows].astype(jnp.bfloat16)
            dft[:, 0:PERIOD] = parts
            dft[:, PERIOD:] = parts
        lax.fori_loop(c * STEP // 8, (c + 1) * STEP // 8, filt, 0, unroll=True)

    between()
    for pair in range(LOCAL // 2):
        highs, lows = [], []
        for i in (2 * pair, 2 * pair + 1):
            x = jnp.concatenate([fir[j, pl.ds(i, SPECTRA, stride=PITCH), :] for j in range(3)], axis=1)
            high = x.astype(jnp.bfloat16)
            highs.append(high)
            lows.append((x - high.astype(jnp.float32)).astype(jnp.bfloat16))
        high, low = jnp.concatenate(highs, axis=0), jnp.concatenate(lows, axis=0)
        right = jnp.concatenate([high, low], axis=1)
        both = lax.dot_general(dft[...], right, (((1,), (1,)), ((), ())), preferred_element_type=jnp.float32)
        out = both[:rows] + both[rows:]
        for half in range(2):
            spec[pl.ds(2 * pair + half, rows, stride=LOCAL), :] = out[:, half * SPECTRA : (half + 1) * SPECTRA]


def equalize(ring, alive, spec, ready):
    for e in range(2 * DEPTH):
        at = pl.multiple_of((ring * 2 * DEPTH + e) * 2 * LOCAL, 2 * LOCAL)
        re, im = spec[pl.ds(at, LOCAL), :], spec[pl.ds(at + LOCAL, LOCAL), :]
        power = jnp.sum(re * re + im * im, axis=1, keepdims=True) * (1.0 / SPECTRA)
        gain = lax.rsqrt(power + 1e-06) * alive
        both = jnp.concatenate([re * gain, im * gain], axis=1)
        ready[ring, e // DEPTH, e % DEPTH] = both.astype(jnp.bfloat16)


def exchange_kernel(
    volts_hbm, table_hbm, mask_hbm, pairs_hbm, out, pairs, volts, table, mask, dft, fir, spec, ready, relay, load, s1, s2, s3, r1, r2, r3, sl
):
    z, x, y, c = place()
    q = lax.rem(x, 2)
    here, own = z * SIDE + y, slot(z, x, y, c)
    other_core = device(z, x, y, 1 - c)
    barrier = pltpu.get_barrier_semaphore()

    def signal(to):
        pl.semaphore_signal(barrier, inc=1, device_id=to, device_id_type=MESH)

    def plane(zd):
        for dy in range(SIDE):
            signal(device(zd, x, ahead(y, dy), c))

    for dy in NEAR:
        signal(device(z, x, ahead(y, dy), c))
    for d in (1, 2, 3):
        signal(device(z, ahead(x, d), y, c))
    signal(other_core)
    for dz in (1, 2, 3):
        pl.when((z > 0) & (ahead(z, dz) > 0))(lambda dz=dz: plane(ahead(z, dz)))

    def greet_first():
        pl.semaphore_wait(barrier, 7)
        for zd in (1, 2, 3):
            plane(zd)

    def greet_others():
        pl.semaphore_wait(barrier, 7 + 3 * SIDE)
        plane(0)

    def between():
        pl.when(z == 0)(greet_first)
        pl.when(z > 1)(greet_others)

    alive_load = pltpu.make_async_copy(mask_hbm, mask, load.at[CHUNKS + 1])
    alive_load.start()
    pairs_load = pltpu.make_async_copy(pairs_hbm, pairs, load.at[CHUNKS + 2])
    pairs_load.start()
    channelize(volts_hbm, table_hbm, volts, table, dft, fir, spec, load, between)
    pl.when(z == 1)(greet_others)
    alive_load.wait()
    inputs = lax.broadcasted_iota(jnp.int32, (LOCAL, 1), 0)
    alive = jnp.zeros((LOCAL, 1), jnp.float32)
    for i in range(LOCAL):
        alive = jnp.where(inputs == i, mask[i].astype(jnp.float32), alive)

    def send(src, dst, send_sem, recv_sem, to):
        pltpu.make_async_remote_copy(
            src_ref=src, dst_ref=dst, send_sem=send_sem, recv_sem=recv_sem, device_id=to, device_id_type=MESH
        ).start()

    def arrived(blocks, sem):
        pltpu.make_async_copy(blocks, blocks, sem).wait()

    def spread(ring, at, mine, others):
        send(mine, out.at[at], s2, r2.at[ring], device(z, ahead(x, 2), y, c))
        send(others, out.at[at], s2, r2.at[ring], device(z, ahead(x, 1), y, c))
        send(others, out.at[at], s2, r2.at[ring], device(z, ahead(x, 3), y, c))
        send(mine, out.at[at], s3, r3, other_core)

    def prepare(dz):
        for dy in ((0,) if dz else ()) + NEAR:
            equalize(ahead(z, dz) * SIDE + ahead(y, dy), alive, spec, ready)

    def depart(zd, offsets=(0,) + NEAR):
        for dy in offsets:
            yd = ahead(y, dy)
            to, there = device(zd, x, yd, c), zd * SIDE + yd
            send(ready.at[there, 1 - q], relay.at[here], s1, r1.at[here], to)
            send(ready.at[there, q], out.at[own], s1, r1.at[here], to)

    def relay_on(zs, offsets=(0,) + NEAR):
        for dy in offsets:
            ys = behind(y, dy)
            ring, at = zs * SIDE + ys, slot(zs, x, ys, c)
            arrived(relay.at[pl.ds(0, 2)], r1.at[ring])
            spread(ring, at, out.at[at], relay.at[ring])

    def hand_over(zs):
        for dy in (0,) + NEAR:
            ys = behind(y, dy)
            arrived(relay.at[pl.ds(0, 3)], r2.at[zs * SIDE + ys])
            for d in (1, 3, 2):
                at = slot(zs, behind(x, d), ys, c)
                send(out.at[at], out.at[at], s3, r3, other_core)

    equalize(here, alive, spec, ready)
    spread(here, own, ready.at[here, q], ready.at[here, 1 - q])
    keep = pltpu.make_async_copy(ready.at[here, q], out.at[own], sl)
    keep.start()
    late = lax.div(z, 3)
    order = [behind(z, dz) for dz in (3 - late, 2 - late, 1 + 2 * late)]
    prepare(0)
    depart(z, NEAR)
    for dz in (3, 2, 1):
        prepare(dz)

    @pl.when(z > 0)
    def _():
        for dz in (3, 2, 1):
            depart(ahead(z, dz))

    relay_on(z, NEAR[:2])

    @pl.when(z == 0)
    def _():
        pl.semaphore_wait(barrier, 3 * SIDE)
        for zd in (3, 2, 1):
            depart(zd)

    relay_on(z, NEAR[2:])
    relay_on(order[0])
    relay_on(order[1])
    hand_over(z)
    relay_on(order[2])
    for zs in order:
        hand_over(zs)
    arrived(out.at[pl.ds(0, 4 * RINGS)], r3)
    arrived(ready.at[pl.ds(0, RINGS - 1)], s1)
    arrived(out.at[pl.ds(0, 3 * RINGS)], s2)
    arrived(out.at[pl.ds(0, 4 * RINGS)], s3)
    keep.wait()
    pairs_load.wait()


def exchange(volts, table, mask, pairs):
    dma = pltpu.SemaphoreType.DMA
    anywhere = pl.BlockSpec(memory_space=pltpu.HBM)
    return pl.pallas_call(
        exchange_kernel,
        out_shape=(
            pltpu.VMEM((128, DEPTH, LOCAL, 2 * SPECTRA), jnp.bfloat16),
            pltpu.SMEM(pairs.shape, pairs.dtype),
        ),
        in_specs=[anywhere] * 4,
        out_specs=(pl.BlockSpec(memory_space=pl.ANY), pl.BlockSpec(memory_space=pl.ANY)),
        scratch_shapes=[
            pltpu.VMEM(volts.shape, jnp.bfloat16),
            pltpu.VMEM(table.shape, jnp.float32),
            pltpu.SMEM(mask.shape, jnp.int32),
            pltpu.VMEM((4 * BAND, 2 * PERIOD), jnp.bfloat16),
            pltpu.VMEM((3, (SPECTRA + 2) * PITCH // 8 * 8, 128), jnp.float32),
            pltpu.VMEM(((2 * BAND + 1) * LOCAL, SPECTRA), jnp.float32),
            pltpu.VMEM((RINGS, 2, DEPTH, LOCAL, 2 * SPECTRA), jnp.bfloat16),
            pltpu.VMEM((RINGS, DEPTH, LOCAL, 2 * SPECTRA), jnp.bfloat16),
            dma((CHUNKS + 4,)),
            dma,
            dma,
            dma,
            dma((RINGS,)),
            dma((RINGS,)),
            dma,
            dma,
        ],
        compiler_params=pltpu.CompilerParams(
            collective_id=0, has_side_effects=True, vmem_limit_bytes=56 * 1024 * 1024
        ),
        cost_estimate=pl.CostEstimate(flops=2 * 3 * 192 * 384 * 2048, bytes_accessed=6 << 20, transcendentals=1536),
        name="exchange",
    )(volts, table, mask, pairs)


def correlate_kernel(table, spectra, out, vis, sem):
    pairs = out.shape[0]

    def pair(row, carry):
        a, b = table[0, row], table[1, row]
        for ch in range(DEPTH):
            left = spectra[pl.ds(a * LOCAL, LOCAL), ch].reshape(BLOCK, 2 * SPECTRA)
            right = spectra[pl.ds(b * LOCAL, LOCAL), ch].reshape(BLOCK, 2 * SPECTRA)
            turned = jnp.concatenate([left[:, SPECTRA:], -left[:, :SPECTRA]], axis=1)
            both = jnp.concatenate([left, turned], axis=0)
            sums = lax.dot_general(both, right, (((1,), (1,)), ((), ())), preferred_element_type=jnp.float32)
            vis[row, ch] = (sums * (1.0 / SPECTRA)).astype(jnp.bfloat16).reshape(2, BLOCK, BLOCK)
            pltpu.make_async_copy(vis.at[row, ch], out.at[row, ch], sem).start()
        return carry

    lax.fori_loop(0, pairs, pair, 0, unroll=True)
    pltpu.make_async_copy(vis, out, sem).wait()


def correlate(table, spectra):
    shape = (table.shape[1], DEPTH, 2, BLOCK, BLOCK)
    return pl.pallas_call(
        correlate_kernel,
        out_shape=jax.ShapeDtypeStruct(shape, jnp.bfloat16),
        in_specs=[pl.BlockSpec(memory_space=pltpu.SMEM), pl.BlockSpec(memory_space=pltpu.VMEM)],
        out_specs=pl.BlockSpec(memory_space=pl.ANY),
        scratch_shapes=[pltpu.VMEM(shape, jnp.bfloat16), pltpu.SemaphoreType.DMA],
        compiler_params=pltpu.CompilerParams(vmem_limit_bytes=32 * 1024 * 1024),
        cost_estimate=pl.CostEstimate(flops=2 * 54 * 256**3, bytes_accessed=10 << 20, transcendentals=0),
        name="correlate",
    )(table, spectra)


def body(voltages, input_alive_mask, pair_table):
    spectra, pairs = exchange(voltages, jnp.asarray(tables()), input_alive_mask, pair_table.T)
    return correlate(pairs, spectra)


def solution(mesh):
    in_specs = (P(("freq", "pair"), None), P(("freq", "pair")), P("pair", None))
    out_specs = P("pair", "freq", None, None, None)
    return jax.shard_map(body, mesh=mesh, in_specs=in_specs, out_specs=out_specs, check_vma=False)
```

```python
import math

import jax
import jax.numpy as jnp
import numpy as np
from jax import lax
from jax.experimental import pallas as pl
from jax.experimental.pallas import tpu as pltpu
from jax.sharding import PartitionSpec as P

CHAN = 192
BAND = 96
TAPS = 4
SPECTRA = 128
BLOCK = 256
PERIOD = 2 * CHAN
SIDE = 4
RINGS = SIDE * SIDE
LOCAL = 16
DEPTH = 3
GROUPS = BAND // DEPTH
MESH = pl.DeviceIdType.MESH

NEAR = (3, 1, 2)


def tables():
    length = TAPS * PERIOD
    j = np.arange(length, dtype=np.float64)
    window = np.sinc((j - length / 2 + 0.5) / PERIOD) * (0.54 - 0.46 * np.cos(2 * math.pi * j / (length - 1)))
    window = window.reshape(TAPS, PERIOD).astype(np.float32)
    z, y, q, ch = np.meshgrid(np.arange(4), np.arange(4), np.arange(2), np.arange(DEPTH), indexing="ij")
    k = ((z * 8 + q * 4 + y) * DEPTH + ch).reshape(-1)
    phase = 2 * math.pi / PERIOD * (k[:, None] * np.arange(PERIOD)[None, :] % PERIOD)
    rows = np.stack([np.cos(phase), -np.sin(phase)], axis=1).reshape(2 * BAND, PERIOD)
    high = rows.astype(jnp.bfloat16).astype(np.float64)
    low = (rows - high).astype(jnp.bfloat16)
    return np.concatenate([high, low.astype(np.float64), window, np.zeros((8 - TAPS, PERIOD))]).astype(np.float32)


def place():
    f, p = lax.axis_index("freq"), lax.axis_index("pair")
    z, x_lo, y = lax.div(f, 8), lax.rem(lax.div(f, 4), 2), lax.rem(f, 4)
    return z, lax.div(p, 2) * 2 + x_lo, y, lax.rem(p, 2)


def device(z, x, y, c):
    return (z * 8 + lax.rem(x, 2) * 4 + y, lax.div(x, 2) * 2 + c)


def slot(z, x, y, c):
    f, p = device(z, x, y, c)
    return f * 4 + p


def ahead(a, d):
    return lax.rem(a + d, SIDE)


def behind(a, d):
    return lax.rem(a + SIDE - d, SIDE)


CHUNKS = 4
STEP = SPECTRA // CHUNKS
PITCH = LOCAL + 1


def chunk(c):
    first = 0 if c == 0 else c * STEP + TAPS - 1
    return pl.ds(first * PERIOD, ((c + 1) * STEP + TAPS - 1 - first) * PERIOD)


def channelize(volts_hbm, table_hbm, volts, table, dft, fir, spec, load, enter, between):
    rows = 2 * BAND
    loads = []
    for c in range(CHUNKS):
        loads.append(pltpu.make_async_copy(volts_hbm.at[:, chunk(c)], volts.at[:, chunk(c)], load.at[c]))
    taps = pltpu.make_async_copy(table_hbm.at[pl.ds(2 * rows, 8)], table.at[pl.ds(2 * rows, 8)], load.at[CHUNKS + 3])
    waves = pltpu.make_async_copy(table_hbm.at[pl.ds(0, 2 * rows)], table.at[pl.ds(0, 2 * rows)], load.at[CHUNKS])
    taps.start()
    loads[0].start()
    loads[1].start()
    waves.start()
    for part in loads[2:]:
        part.start()
    enter()
    taps.wait()

    def filt(step, carry):
        first = step * 8
        frames = []
        for t in range(8 + TAPS - 1):
            at = pl.multiple_of((first + t) * PERIOD, 128)
            frames.append(volts[:, pl.ds(at, PERIOD)].astype(jnp.float32))
        window = [table[2 * rows + m : 2 * rows + m + 1, :] for m in range(TAPS)]
        for t in range(8):
            total = window[0] * frames[t]
            for m in range(1, TAPS):
                total = total + window[m] * frames[t + m]
            row = (first + t) * PITCH
            for j in range(3):
                fir[j, pl.ds(row, LOCAL), :] = total[:, j * 128 : (j + 1) * 128]
        return carry

    for c in range(CHUNKS):
        loads[c].wait()
        if c == CHUNKS - 1:
            waves.wait()
            parts = table[0 : 2 * rows].astype(jnp.bfloat16)
            dft[:, 0:PERIOD] = parts
            dft[:, PERIOD:] = parts
        lax.fori_loop(c * STEP // 8, (c + 1) * STEP // 8, filt, 0, unroll=True)

    between()
    for pair in range(LOCAL // 2):
        highs, lows = [], []
        for i in (2 * pair, 2 * pair + 1):
            x = jnp.concatenate([fir[j, pl.ds(i, SPECTRA, stride=PITCH), :] for j in range(3)], axis=1)
            high = x.astype(jnp.bfloat16)
            highs.append(high)
            lows.append((x - high.astype(jnp.float32)).astype(jnp.bfloat16))
        high, low = jnp.concatenate(highs, axis=0), jnp.concatenate(lows, axis=0)
        right = jnp.concatenate([high, low], axis=1)
        both = lax.dot_general(dft[...], right, (((1,), (1,)), ((), ())), preferred_element_type=jnp.float32)
        out = both[:rows] + both[rows:]
        for half in range(2):
            spec[pl.ds(2 * pair + half, rows, stride=LOCAL), :] = out[:, half * SPECTRA : (half + 1) * SPECTRA]


def equalize(ring, alive, spec, ready):
    for e in range(2 * DEPTH):
        at = pl.multiple_of((ring * 2 * DEPTH + e) * 2 * LOCAL, 2 * LOCAL)
        re, im = spec[pl.ds(at, LOCAL), :], spec[pl.ds(at + LOCAL, LOCAL), :]
        power = jnp.sum(re * re + im * im, axis=1, keepdims=True) * (1.0 / SPECTRA)
        gain = lax.rsqrt(power + 1e-06) * alive
        both = jnp.concatenate([re * gain, im * gain], axis=1)
        ready[ring, e // DEPTH, e % DEPTH] = both.astype(jnp.bfloat16)


def exchange_kernel(
    volts_hbm, table_hbm, mask_hbm, pairs_hbm, out, pairs, volts, table, mask, dft, fir, spec, ready, relay, load, s1, s2, s3, r1, r2, r3, sl
):
    z, x, y, c = place()
    q = lax.rem(x, 2)
    here, own = z * SIDE + y, slot(z, x, y, c)
    other_core = device(z, x, y, 1 - c)
    barrier = pltpu.get_barrier_semaphore()

    def signal(to):
        pl.semaphore_signal(barrier, inc=1, device_id=to, device_id_type=MESH)

    def plane(zd):
        for dy in range(SIDE):
            signal(device(zd, x, ahead(y, dy), c))

    def enter():
        for dy in NEAR:
            signal(device(z, x, ahead(y, dy), c))
        for d in (1, 2, 3):
            signal(device(z, ahead(x, d), y, c))
        signal(other_core)
        for dz in (1, 2, 3):
            pl.when((z > 0) & (ahead(z, dz) > 0))(lambda dz=dz: plane(ahead(z, dz)))

    def greet_first():
        pl.semaphore_wait(barrier, 7)
        for zd in (1, 2, 3):
            plane(zd)

    def greet_others():
        pl.semaphore_wait(barrier, 7 + 3 * SIDE)
        plane(0)

    def between():
        pl.when(z == 0)(greet_first)
        pl.when(z > 1)(greet_others)

    alive_load = pltpu.make_async_copy(mask_hbm, mask, load.at[CHUNKS + 1])
    alive_load.start()
    pairs_load = pltpu.make_async_copy(pairs_hbm, pairs, load.at[CHUNKS + 2])
    pairs_load.start()
    channelize(volts_hbm, table_hbm, volts, table, dft, fir, spec, load, enter, between)
    pl.when(z == 1)(greet_others)
    alive_load.wait()
    inputs = lax.broadcasted_iota(jnp.int32, (LOCAL, 1), 0)
    alive = jnp.zeros((LOCAL, 1), jnp.float32)
    for i in range(LOCAL):
        alive = jnp.where(inputs == i, mask[i].astype(jnp.float32), alive)

    def send(src, dst, send_sem, recv_sem, to):
        pltpu.make_async_remote_copy(
            src_ref=src, dst_ref=dst, send_sem=send_sem, recv_sem=recv_sem, device_id=to, device_id_type=MESH
        ).start()

    def arrived(blocks, sem):
        pltpu.make_async_copy(blocks, blocks, sem).wait()

    def spread(ring, at, mine, others):
        send(mine, out.at[at], s2, r2.at[ring], device(z, ahead(x, 2), y, c))
        send(others, out.at[at], s2, r2.at[ring], device(z, ahead(x, 1), y, c))
        send(others, out.at[at], s2, r2.at[ring], device(z, ahead(x, 3), y, c))
        send(mine, out.at[at], s3, r3, other_core)

    def prepare(dz):
        for dy in ((0,) if dz else ()) + NEAR:
            equalize(ahead(z, dz) * SIDE + ahead(y, dy), alive, spec, ready)

    def depart(zd, offsets=(0,) + NEAR):
        for dy in offsets:
            yd = ahead(y, dy)
            to, there = device(zd, x, yd, c), zd * SIDE + yd
            send(ready.at[there, 1 - q], relay.at[here], s1, r1.at[here], to)
            send(ready.at[there, q], out.at[own], s1, r1.at[here], to)

    def relay_on(zs, offsets=(0,) + NEAR):
        for dy in offsets:
            ys = behind(y, dy)
            ring, at = zs * SIDE + ys, slot(zs, x, ys, c)
            arrived(relay.at[pl.ds(0, 2)], r1.at[ring])
            spread(ring, at, out.at[at], relay.at[ring])

    def hand_over(zs):
        for dy in (0,) + NEAR:
            ys = behind(y, dy)
            arrived(relay.at[pl.ds(0, 3)], r2.at[zs * SIDE + ys])
            for d in (1, 3, 2):
                at = slot(zs, behind(x, d), ys, c)
                send(out.at[at], out.at[at], s3, r3, other_core)

    equalize(here, alive, spec, ready)
    spread(here, own, ready.at[here, q], ready.at[here, 1 - q])
    keep = pltpu.make_async_copy(ready.at[here, q], out.at[own], sl)
    keep.start()
    late = lax.div(z, 3)
    order = [behind(z, dz) for dz in (3 - late, 2 - late, 1 + 2 * late)]
    prepare(0)
    depart(z, NEAR)
    for dz in (3, 2, 1):
        prepare(dz)

    @pl.when(z > 0)
    def _():
        for dz in (3, 2, 1):
            depart(ahead(z, dz))

    relay_on(z, NEAR[:2])

    @pl.when(z == 0)
    def _():
        pl.semaphore_wait(barrier, 3 * SIDE)
        for zd in (3, 2, 1):
            depart(zd)

    relay_on(z, NEAR[2:])
    relay_on(order[0])
    relay_on(order[1])
    hand_over(z)
    relay_on(order[2])
    for zs in order:
        hand_over(zs)
    arrived(out.at[pl.ds(0, 4 * RINGS)], r3)
    arrived(ready.at[pl.ds(0, RINGS - 1)], s1)
    arrived(out.at[pl.ds(0, 3 * RINGS)], s2)
    arrived(out.at[pl.ds(0, 4 * RINGS)], s3)
    keep.wait()
    pairs_load.wait()


def exchange(volts, table, mask, pairs):
    dma = pltpu.SemaphoreType.DMA
    anywhere = pl.BlockSpec(memory_space=pltpu.HBM)
    return pl.pallas_call(
        exchange_kernel,
        out_shape=(
            pltpu.VMEM((128, DEPTH, LOCAL, 2 * SPECTRA), jnp.bfloat16),
            pltpu.SMEM(pairs.shape, pairs.dtype),
        ),
        in_specs=[anywhere] * 4,
        out_specs=(pl.BlockSpec(memory_space=pl.ANY), pl.BlockSpec(memory_space=pl.ANY)),
        scratch_shapes=[
            pltpu.VMEM(volts.shape, jnp.bfloat16),
            pltpu.VMEM(table.shape, jnp.float32),
            pltpu.SMEM(mask.shape, jnp.int32),
            pltpu.VMEM((4 * BAND, 2 * PERIOD), jnp.bfloat16),
            pltpu.VMEM((3, (SPECTRA + 2) * PITCH // 8 * 8, 128), jnp.float32),
            pltpu.VMEM(((2 * BAND + 1) * LOCAL, SPECTRA), jnp.float32),
            pltpu.VMEM((RINGS, 2, DEPTH, LOCAL, 2 * SPECTRA), jnp.bfloat16),
            pltpu.VMEM((RINGS, DEPTH, LOCAL, 2 * SPECTRA), jnp.bfloat16),
            dma((CHUNKS + 4,)),
            dma,
            dma,
            dma,
            dma((RINGS,)),
            dma((RINGS,)),
            dma,
            dma,
        ],
        compiler_params=pltpu.CompilerParams(
            collective_id=0, has_side_effects=True, vmem_limit_bytes=56 * 1024 * 1024
        ),
        cost_estimate=pl.CostEstimate(flops=2 * 3 * 192 * 384 * 2048, bytes_accessed=6 << 20, transcendentals=1536),
        name="exchange",
    )(volts, table, mask, pairs)


def correlate_kernel(table, spectra, out, vis, sem):
    pairs = out.shape[0]

    def pair(row, carry):
        a, b = table[0, row], table[1, row]
        for ch in range(DEPTH):
            left = spectra[pl.ds(a * LOCAL, LOCAL), ch].reshape(BLOCK, 2 * SPECTRA)
            right = spectra[pl.ds(b * LOCAL, LOCAL), ch].reshape(BLOCK, 2 * SPECTRA)
            turned = jnp.concatenate([left[:, SPECTRA:], -left[:, :SPECTRA]], axis=1)
            both = jnp.concatenate([left, turned], axis=0)
            sums = lax.dot_general(both, right, (((1,), (1,)), ((), ())), preferred_element_type=jnp.float32)
            vis[row, ch] = (sums * (1.0 / SPECTRA)).astype(jnp.bfloat16).reshape(2, BLOCK, BLOCK)
            pltpu.make_async_copy(vis.at[row, ch], out.at[row, ch], sem).start()
        return carry

    lax.fori_loop(0, pairs, pair, 0, unroll=True)
    pltpu.make_async_copy(vis, out, sem).wait()


def correlate(table, spectra):
    shape = (table.shape[1], DEPTH, 2, BLOCK, BLOCK)
    return pl.pallas_call(
        correlate_kernel,
        out_shape=jax.ShapeDtypeStruct(shape, jnp.bfloat16),
        in_specs=[pl.BlockSpec(memory_space=pltpu.SMEM), pl.BlockSpec(memory_space=pltpu.VMEM)],
        out_specs=pl.BlockSpec(memory_space=pl.ANY),
        scratch_shapes=[pltpu.VMEM(shape, jnp.bfloat16), pltpu.SemaphoreType.DMA],
        compiler_params=pltpu.CompilerParams(vmem_limit_bytes=32 * 1024 * 1024),
        cost_estimate=pl.CostEstimate(flops=2 * 54 * 256**3, bytes_accessed=10 << 20, transcendentals=0),
        name="correlate",
    )(table, spectra)


def body(voltages, input_alive_mask, pair_table):
    spectra, pairs = exchange(voltages, jnp.asarray(tables()), input_alive_mask, pair_table.T)
    return correlate(pairs, spectra)


def solution(mesh):
    in_specs = (P(("freq", "pair"), None), P(("freq", "pair")), P("pair", None))
    out_specs = P("pair", "freq", None, None, None)
    return jax.shard_map(body, mesh=mesh, in_specs=in_specs, out_specs=out_specs, check_vma=False)
```

```python
import math

import jax
import jax.numpy as jnp
import numpy as np
from jax import lax
from jax.experimental import pallas as pl
from jax.experimental.pallas import tpu as pltpu
from jax.sharding import PartitionSpec as P

CHAN = 192
BAND = 96
TAPS = 4
SPECTRA = 128
BLOCK = 256
PERIOD = 2 * CHAN
SIDE = 4
RINGS = SIDE * SIDE
LOCAL = 16
DEPTH = 3
GROUPS = BAND // DEPTH
MESH = pl.DeviceIdType.MESH

NEAR = (3, 1, 2)


def tables():
    length = TAPS * PERIOD
    j = np.arange(length, dtype=np.float64)
    window = np.sinc((j - length / 2 + 0.5) / PERIOD) * (0.54 - 0.46 * np.cos(2 * math.pi * j / (length - 1)))
    window = window.reshape(TAPS, PERIOD).astype(np.float32)
    z, y, q, ch = np.meshgrid(np.arange(4), np.arange(4), np.arange(2), np.arange(DEPTH), indexing="ij")
    k = ((z * 8 + q * 4 + y) * DEPTH + ch).reshape(-1)
    phase = 2 * math.pi / PERIOD * (k[:, None] * np.arange(PERIOD)[None, :] % PERIOD)
    rows = np.stack([np.cos(phase), -np.sin(phase)], axis=1).reshape(2 * BAND, PERIOD)
    high = rows.astype(jnp.bfloat16).astype(np.float64)
    low = (rows - high).astype(jnp.bfloat16)
    return np.concatenate([high, low.astype(np.float64), window, np.zeros((8 - TAPS, PERIOD))]).astype(np.float32)


def place():
    f, p = lax.axis_index("freq"), lax.axis_index("pair")
    z, x_lo, y = lax.div(f, 8), lax.rem(lax.div(f, 4), 2), lax.rem(f, 4)
    return z, lax.div(p, 2) * 2 + x_lo, y, lax.rem(p, 2)


def device(z, x, y, c):
    return (z * 8 + lax.rem(x, 2) * 4 + y, lax.div(x, 2) * 2 + c)


def slot(z, x, y, c):
    f, p = device(z, x, y, c)
    return f * 4 + p


def ahead(a, d):
    return lax.rem(a + d, SIDE)


def behind(a, d):
    return lax.rem(a + SIDE - d, SIDE)


CHUNKS = 4
STEP = SPECTRA // CHUNKS
PITCH = LOCAL + 1


def chunk(c):
    first = 0 if c == 0 else c * STEP + TAPS - 1
    return pl.ds(first * PERIOD, ((c + 1) * STEP + TAPS - 1 - first) * PERIOD)


def channelize(volts_hbm, table_hbm, volts, table, dft, fir, spec, load, enter, between):
    rows = 2 * BAND
    loads = []
    for c in range(CHUNKS):
        loads.append(pltpu.make_async_copy(volts_hbm.at[:, chunk(c)], volts.at[:, chunk(c)], load.at[c]))
    taps = pltpu.make_async_copy(table_hbm.at[pl.ds(2 * rows, 8)], table.at[pl.ds(2 * rows, 8)], load.at[CHUNKS + 3])
    waves = pltpu.make_async_copy(table_hbm.at[pl.ds(0, 2 * rows)], table.at[pl.ds(0, 2 * rows)], load.at[CHUNKS])
    taps.start()
    loads[0].start()
    loads[1].start()
    waves.start()
    for part in loads[2:]:
        part.start()
    enter()
    taps.wait()

    def filt(step, carry):
        first = step * 8
        frames = []
        for t in range(8 + TAPS - 1):
            at = pl.multiple_of((first + t) * PERIOD, 128)
            frames.append(volts[:, pl.ds(at, PERIOD)].astype(jnp.float32))
        window = [table[2 * rows + m : 2 * rows + m + 1, :] for m in range(TAPS)]
        for t in range(8):
            total = window[0] * frames[t]
            for m in range(1, TAPS):
                total = total + window[m] * frames[t + m]
            row = (first + t) * PITCH
            for j in range(3):
                fir[j, pl.ds(row, LOCAL), :] = total[:, j * 128 : (j + 1) * 128]
        return carry

    for c in range(CHUNKS):
        loads[c].wait()
        if c == CHUNKS - 1:
            waves.wait()
            parts = table[0 : 2 * rows].astype(jnp.bfloat16)
            dft[:, 0:PERIOD] = parts
            dft[:, PERIOD:] = parts
        lax.fori_loop(c * STEP // 8, (c + 1) * STEP // 8, filt, 0, unroll=True)

    between()
    for pair in range(LOCAL // 2):
        highs, lows = [], []
        for i in (2 * pair, 2 * pair + 1):
            x = jnp.concatenate([fir[j, pl.ds(i, SPECTRA, stride=PITCH), :] for j in range(3)], axis=1)
            high = x.astype(jnp.bfloat16)
            highs.append(high)
            lows.append((x - high.astype(jnp.float32)).astype(jnp.bfloat16))
        high, low = jnp.concatenate(highs, axis=0), jnp.concatenate(lows, axis=0)
        right = jnp.concatenate([high, low], axis=1)
        both = lax.dot_general(dft[...], right, (((1,), (1,)), ((), ())), preferred_element_type=jnp.float32)
        out = both[:rows] + both[rows:]
        for half in range(2):
            spec[pl.ds(2 * pair + half, rows, stride=LOCAL), :] = out[:, half * SPECTRA : (half + 1) * SPECTRA]


def equalize(ring, alive, spec, ready):
    for e in range(2 * DEPTH):
        at = pl.multiple_of((ring * 2 * DEPTH + e) * 2 * LOCAL, 2 * LOCAL)
        re, im = spec[pl.ds(at, LOCAL), :], spec[pl.ds(at + LOCAL, LOCAL), :]
        power = jnp.sum(re * re + im * im, axis=1, keepdims=True) * (1.0 / SPECTRA)
        gain = lax.rsqrt(power + 1e-06) * alive
        both = jnp.concatenate([re * gain, im * gain], axis=1)
        ready[ring, e // DEPTH, e % DEPTH] = both.astype(jnp.bfloat16)


def exchange_kernel(
    volts_hbm, table_hbm, mask_hbm, pairs_hbm, out, pairs, volts, table, mask, dft, fir, spec, ready, relay, load, s1, s2, s3, r1, r2, r3, sl
):
    z, x, y, c = place()
    q = lax.rem(x, 2)
    here, own = z * SIDE + y, slot(z, x, y, c)
    other_core = device(z, x, y, 1 - c)
    barrier = pltpu.get_barrier_semaphore()

    def signal(to):
        pl.semaphore_signal(barrier, inc=1, device_id=to, device_id_type=MESH)

    def plane(zd):
        for dy in range(SIDE):
            signal(device(zd, x, ahead(y, dy), c))

    def enter():
        for dy in NEAR:
            signal(device(z, x, ahead(y, dy), c))
        for d in (1, 2, 3):
            signal(device(z, ahead(x, d), y, c))
        signal(other_core)
        for dz in (1, 2, 3):
            pl.when((z > 0) & (ahead(z, dz) > 0))(lambda dz=dz: plane(ahead(z, dz)))

    def greet_first():
        pl.semaphore_wait(barrier, 7)
        for zd in (1, 2, 3):
            plane(zd)

    def greet_others():
        pl.semaphore_wait(barrier, 7 + 3 * SIDE)
        plane(0)

    def between():
        pl.when(z == 0)(greet_first)
        pl.when((z > 1) & (y > 1))(greet_others)

    alive_load = pltpu.make_async_copy(mask_hbm, mask, load.at[CHUNKS + 1])
    alive_load.start()
    pairs_load = pltpu.make_async_copy(pairs_hbm, pairs, load.at[CHUNKS + 2])
    pairs_load.start()
    channelize(volts_hbm, table_hbm, volts, table, dft, fir, spec, load, enter, between)
    pl.when((z == 1) | ((z > 1) & (y < 2)))(greet_others)
    alive_load.wait()
    inputs = lax.broadcasted_iota(jnp.int32, (LOCAL, 1), 0)
    alive = jnp.zeros((LOCAL, 1), jnp.float32)
    for i in range(LOCAL):
        alive = jnp.where(inputs == i, mask[i].astype(jnp.float32), alive)

    def send(src, dst, send_sem, recv_sem, to):
        pltpu.make_async_remote_copy(
            src_ref=src, dst_ref=dst, send_sem=send_sem, recv_sem=recv_sem, device_id=to, device_id_type=MESH
        ).start()

    def arrived(blocks, sem):
        pltpu.make_async_copy(blocks, blocks, sem).wait()

    def spread(ring, at, mine, others):
        send(mine, out.at[at], s2, r2.at[ring], device(z, ahead(x, 2), y, c))
        send(others, out.at[at], s2, r2.at[ring], device(z, ahead(x, 1), y, c))
        send(others, out.at[at], s2, r2.at[ring], device(z, ahead(x, 3), y, c))
        send(mine, out.at[at], s3, r3, other_core)

    def prepare(dz):
        for dy in ((0,) if dz else ()) + NEAR:
            equalize(ahead(z, dz) * SIDE + ahead(y, dy), alive, spec, ready)

    def depart(zd, offsets=(0,) + NEAR):
        for dy in offsets:
            yd = ahead(y, dy)
            to, there = device(zd, x, yd, c), zd * SIDE + yd
            send(ready.at[there, 1 - q], relay.at[here], s1, r1.at[here], to)
            send(ready.at[there, q], out.at[own], s1, r1.at[here], to)

    def relay_on(zs, offsets=(0,) + NEAR):
        for dy in offsets:
            ys = behind(y, dy)
            ring, at = zs * SIDE + ys, slot(zs, x, ys, c)
            arrived(relay.at[pl.ds(0, 2)], r1.at[ring])
            spread(ring, at, out.at[at], relay.at[ring])

    def hand_over(zs):
        for dy in (0,) + NEAR:
            ys = behind(y, dy)
            arrived(relay.at[pl.ds(0, 3)], r2.at[zs * SIDE + ys])
            for d in (1, 3, 2):
                at = slot(zs, behind(x, d), ys, c)
                send(out.at[at], out.at[at], s3, r3, other_core)

    equalize(here, alive, spec, ready)
    spread(here, own, ready.at[here, q], ready.at[here, 1 - q])
    keep = pltpu.make_async_copy(ready.at[here, q], out.at[own], sl)
    keep.start()
    late = lax.div(z, 3)
    order = [behind(z, dz) for dz in (3 - late, 2 - late, 1 + 2 * late)]
    prepare(0)
    depart(z, NEAR)
    for dz in (3, 2, 1):
        prepare(dz)

    @pl.when(z > 0)
    def _():
        for dz in (3, 2, 1):
            depart(ahead(z, dz))

    relay_on(z, NEAR[:2])

    @pl.when(z == 0)
    def _():
        pl.semaphore_wait(barrier, 3 * SIDE)
        for zd in (3, 2, 1):
            depart(zd)

    relay_on(z, NEAR[2:])
    relay_on(order[0])
    relay_on(order[1])
    hand_over(z)
    relay_on(order[2])
    for zs in order:
        hand_over(zs)
    arrived(out.at[pl.ds(0, 4 * RINGS)], r3)
    arrived(ready.at[pl.ds(0, RINGS - 1)], s1)
    arrived(out.at[pl.ds(0, 3 * RINGS)], s2)
    arrived(out.at[pl.ds(0, 4 * RINGS)], s3)
    keep.wait()
    pairs_load.wait()


def exchange(volts, table, mask, pairs):
    dma = pltpu.SemaphoreType.DMA
    anywhere = pl.BlockSpec(memory_space=pltpu.HBM)
    return pl.pallas_call(
        exchange_kernel,
        out_shape=(
            pltpu.VMEM((128, DEPTH, LOCAL, 2 * SPECTRA), jnp.bfloat16),
            pltpu.SMEM(pairs.shape, pairs.dtype),
        ),
        in_specs=[anywhere] * 4,
        out_specs=(pl.BlockSpec(memory_space=pl.ANY), pl.BlockSpec(memory_space=pl.ANY)),
        scratch_shapes=[
            pltpu.VMEM(volts.shape, jnp.bfloat16),
            pltpu.VMEM(table.shape, jnp.float32),
            pltpu.SMEM(mask.shape, jnp.int32),
            pltpu.VMEM((4 * BAND, 2 * PERIOD), jnp.bfloat16),
            pltpu.VMEM((3, (SPECTRA + 2) * PITCH // 8 * 8, 128), jnp.float32),
            pltpu.VMEM(((2 * BAND + 1) * LOCAL, SPECTRA), jnp.float32),
            pltpu.VMEM((RINGS, 2, DEPTH, LOCAL, 2 * SPECTRA), jnp.bfloat16),
            pltpu.VMEM((RINGS, DEPTH, LOCAL, 2 * SPECTRA), jnp.bfloat16),
            dma((CHUNKS + 4,)),
            dma,
            dma,
            dma,
            dma((RINGS,)),
            dma((RINGS,)),
            dma,
            dma,
        ],
        compiler_params=pltpu.CompilerParams(
            collective_id=0, has_side_effects=True, vmem_limit_bytes=56 * 1024 * 1024
        ),
        cost_estimate=pl.CostEstimate(flops=2 * 3 * 192 * 384 * 2048, bytes_accessed=6 << 20, transcendentals=1536),
        name="exchange",
    )(volts, table, mask, pairs)


def correlate_kernel(table, spectra, out, vis, sem):
    pairs = out.shape[0]

    def pair(row, carry):
        a, b = table[0, row], table[1, row]
        for ch in range(DEPTH):
            left = spectra[pl.ds(a * LOCAL, LOCAL), ch].reshape(BLOCK, 2 * SPECTRA)
            right = spectra[pl.ds(b * LOCAL, LOCAL), ch].reshape(BLOCK, 2 * SPECTRA)
            turned = jnp.concatenate([left[:, SPECTRA:], -left[:, :SPECTRA]], axis=1)
            both = jnp.concatenate([left, turned], axis=0)
            sums = lax.dot_general(both, right, (((1,), (1,)), ((), ())), preferred_element_type=jnp.float32)
            vis[row, ch] = (sums * (1.0 / SPECTRA)).astype(jnp.bfloat16).reshape(2, BLOCK, BLOCK)
            pltpu.make_async_copy(vis.at[row, ch], out.at[row, ch], sem).start()
        return carry

    lax.fori_loop(0, pairs, pair, 0, unroll=True)
    pltpu.make_async_copy(vis, out, sem).wait()


def correlate(table, spectra):
    shape = (table.shape[1], DEPTH, 2, BLOCK, BLOCK)
    return pl.pallas_call(
        correlate_kernel,
        out_shape=jax.ShapeDtypeStruct(shape, jnp.bfloat16),
        in_specs=[pl.BlockSpec(memory_space=pltpu.SMEM), pl.BlockSpec(memory_space=pltpu.VMEM)],
        out_specs=pl.BlockSpec(memory_space=pl.ANY),
        scratch_shapes=[pltpu.VMEM(shape, jnp.bfloat16), pltpu.SemaphoreType.DMA],
        compiler_params=pltpu.CompilerParams(vmem_limit_bytes=32 * 1024 * 1024),
        cost_estimate=pl.CostEstimate(flops=2 * 54 * 256**3, bytes_accessed=10 << 20, transcendentals=0),
        name="correlate",
    )(table, spectra)


def body(voltages, input_alive_mask, pair_table):
    spectra, pairs = exchange(voltages, jnp.asarray(tables()), input_alive_mask, pair_table.T)
    return correlate(pairs, spectra)


def solution(mesh):
    in_specs = (P(("freq", "pair"), None), P(("freq", "pair")), P("pair", None))
    out_specs = P("pair", "freq", None, None, None)
    return jax.shard_map(body, mesh=mesh, in_specs=in_specs, out_specs=out_specs, check_vma=False)
```
